32 devices in a mesh: dp: 8 (over z, x), dim: 4 (over y, core).
Axes of the slice: x: 2, y: 2, z: 4, core: 2. Of those that a mesh axis runs over, the one named last changes fastest.
Arguments:
- vectors: bfloat16 [768, 8192], P('dim', 'dp'), may hold values from -30 to 30
- codes: int32 [64, 8192], P('dim', 'dp'), may hold values from 0 to 255, as said below
- codebook: bfloat16 [256, 768], P(None, 'dim'), may hold values from -4 to 4
Outputs:
- rotation: float32 [768, 768], P('dim')
- new_codebook: float32 [256, 768], P('dp', 'dim')
The draws below stay inside these ranges and needn't reach their ends.
Inputs may be any that keep to these rules, and one draw needn't show every extreme that they name: `codes`: each entry names a centroid of its subspace; in each subspace at least one centroid, which one is drawn from the seed, is named by no vector.
All inputs are finite; a program needn't handle non-finite values.
Results may differ from the reference program's by a relative error of at most 0.003.
Values may be sent and summed in bfloat16 or wider, within the bound.
No kernel may reach another device: no remote copies, remote signals or barrier semaphores. Data moves between devices by JAX's collectives and lax.ppermute only.
A program may use at most 64 MiB of HBM per device.

```python
import math
import jax
import jax.numpy as jnp
from jax import lax

D = 768
M = 64
K = 256
NS_STEPS = 4
ROWS = 8192


def code_table(key):
    base = jax.random.fold_in(key, 701)
    unused = jax.random.randint(jax.random.fold_in(base, 1), (M, 1), 0, K)
    offsets = jax.random.randint(jax.random.fold_in(base, 2), (M, ROWS), 0, K - 1)
    return ((unused + 1 + offsets) % K).astype(jnp.int32)


def book_table(key):
    base = jax.random.fold_in(key, 702)
    values = jnp.clip(jax.random.normal(jax.random.fold_in(base, 3), (K, D), jnp.float32), -4.0, 4.0)
    return values.astype(jnp.bfloat16).astype(jnp.float32)


def draw_codes(key, part):
    return code_table(key)


def draw_codebook(key, part):
    return book_table(key).astype(jnp.bfloat16)


def draw_vectors(key, part):
    code_rows = code_table(key)
    book = book_table(key)
    index_rows = jnp.repeat(code_rows, D // M, axis=0)
    decoded = jnp.take_along_axis(book.T, index_rows, axis=1)
    scale_key = jax.random.fold_in(key, 703)
    noise_key = jax.random.fold_in(key, 704)
    feature_scale = jnp.exp(jax.random.uniform(scale_key, (D, 1), jnp.float32, math.log(0.2), math.log(5.0)))
    noise = jnp.clip(jax.random.normal(noise_key, (D, ROWS), jnp.float32), -4.0, 4.0)
    return (feature_scale * (0.5 * decoded + noise)).astype(jnp.bfloat16)


def setup_inputs(seed: int = 0) -> dict:
    splits = jax.random.split(jax.random.key(seed), 4)
    return {
        "vectors": draw_vectors(jax.random.fold_in(splits[3], 71), 0),
        "codes": draw_codes(jax.random.fold_in(splits[3], 71), 0),
        "codebook": draw_codebook(jax.random.fold_in(splits[3], 71), 0),
    }


def reference(vectors, codes, codebook):
    sub_width = D // M
    book_cube = codebook.reshape(K, M, sub_width)
    selected = book_cube[codes.T, jnp.arange(M, dtype=jnp.int32)[None, :]]
    decoded = selected.reshape(ROWS, D)
    cross = jnp.dot(vectors, decoded, preferred_element_type=jnp.float32)
    magnitude = jnp.sqrt(jnp.sum(cross * cross))
    current = cross.T / magnitude
    for iteration in range(NS_STEPS):
        gram_full = jnp.dot(current, current.T, precision=lax.Precision.HIGHEST)
        current = 1.5 * current - 0.5 * jnp.dot(gram_full, current, precision=lax.Precision.HIGHEST)
    rotation = current
    rotation_low = rotation.astype(jnp.bfloat16)
    rotated = jnp.dot(vectors.T, rotation_low.T, preferred_element_type=jnp.float32).astype(jnp.bfloat16)
    slabs = jnp.transpose(rotated.reshape(ROWS, M, sub_width), (1, 0, 2))

    def refit(operands):
        slab_rows, code_row = operands
        totals = jax.ops.segment_sum(slab_rows.astype(jnp.float32), code_row, num_segments=K)
        tallies = jax.ops.segment_sum(jnp.ones((ROWS,), jnp.float32), code_row, num_segments=K)
        return (totals, tallies)
    centroid_sums, counts = lax.map(refit, (slabs, codes))
    centroid_sums = jnp.transpose(centroid_sums, (1, 0, 2)).reshape(K, D)
    counts = jnp.repeat(counts.T, sub_width, axis=1)
    new_codebook = centroid_sums / jnp.maximum(counts, 1.0)
    return (rotation, new_codebook)
```

```python
import functools

import jax
import jax.numpy as jnp
from jax import lax
from jax.experimental import pallas as pl
from jax.experimental.pallas import tpu as pltpu
from jax.sharding import PartitionSpec as P

NS_STEPS = 4
DIMS = 4
LANES = 128
VMEM_LIMIT = 56 * 1024 * 1024


def swap(value, mask):
    count = lax.axis_size("dp") * lax.axis_size("dim")
    return lax.ppermute(value, ("dp", "dim"), [(i, i ^ mask) for i in range(count)])


def place():
    dim = lax.axis_index("dim")
    dp = lax.axis_index("dp")
    return dim & 1, dim >> 1, dp & 3, dp >> 2


def split(value):
    high = value.astype(jnp.bfloat16)
    low = (value - high.astype(jnp.float32)).astype(jnp.bfloat16)
    return high, low


def dot_t(a, b):
    return lax.dot_general(a, b, (((1,), (1,)), ((), ())), preferred_element_type=jnp.float32)


def dot(a, b):
    return jnp.dot(a, b, preferred_element_type=jnp.float32)


def decode(codes_ref, book_ref, sub_width, write):
    sub_count, row_count = codes_ref.shape
    width = sub_count * sub_width
    sublane = lax.broadcasted_iota(jnp.int32, (8, row_count), 0)
    for first in range(0, width, 8):
        one, two = first // sub_width, (first + 7) // sub_width
        index = jnp.broadcast_to(codes_ref[one : one + 1, :], (8, row_count))
        if two != one:
            later = jnp.broadcast_to(codes_ref[two : two + 1, :], (8, row_count))
            index = jnp.where(sublane < two * sub_width - first, index, later)
        book = book_ref[first : first + 8, :].astype(jnp.float32)
        parts = []
        for start in range(0, row_count, LANES):
            at = index[:, start : start + LANES]
            inner = at & (LANES - 1)
            value = jnp.take_along_axis(book[:, :LANES], inner, axis=1, mode="promise_in_bounds")
            for level in range(LANES, book.shape[1], LANES):
                other = jnp.take_along_axis(
                    book[:, level : level + LANES], inner, axis=1, mode="promise_in_bounds"
                )
                value = jnp.where(at >= level, other, value)
            parts.append(value)
        write(first, jnp.concatenate(parts, axis=1))


def cross_kernel(sub_width, v0, v1, code0, code1, book0, book1, *rest):
    outs, (vectors, decoded32) = rest[:4], rest[4:]
    core, pair, quarter, _ = place()
    width = v0.shape[0]
    vectors[pl.ds(pl.multiple_of(core * width, 16), width), :] = v0[...]
    vectors[pl.ds(pl.multiple_of((1 - core) * width, 16), width), :] = v1[...]

    def writer(base):
        def write(row, rows):
            decoded32[pl.ds(pl.multiple_of(base + row, 8), 8), :] = rows

        return write

    decode(code0, book0, sub_width, writer(pair * width))
    decode(code1, book1, sub_width, writer((1 - pair) * width))
    thin = width // 2
    for k, out in enumerate(outs):
        rows = decoded32[pl.ds(pl.multiple_of((quarter ^ k) * thin, 8), thin), :]
        out[...] = dot_t(rows.astype(jnp.bfloat16), vectors[...])


def refit_kernel(sub_width, *refs):
    pieces, (v0, v1, v2, v3, codes) = refs[:16], refs[16:21]
    rotation_out, outs = refs[21], refs[22:26]
    current, high_ref, low_ref, vectors, rotated, total = refs[26:]
    core, pair, quarter, high_part = place()
    dp_count = lax.axis_size("dp")
    thin, half = pieces[0].shape
    width = 2 * thin
    own = (pair * 2 + core) * width

    for mask, piece in enumerate(pieces):
        c, p, q = core ^ (mask & 1), pair ^ (mask >> 1 & 1), quarter ^ (mask >> 2)
        row = ((q >> 1) * 2 + c) * width + (q & 1) * thin
        current[p, pl.ds(pl.multiple_of(row, 8), thin), :] = piece[...]
    for k, v in enumerate((v0, v1, v2, v3)):
        at = ((pair ^ (k >> 1)) * 2 + (core ^ (k & 1))) * width
        vectors[pl.ds(pl.multiple_of(at, 16), width), :] = v[...]

    magnitude = jnp.sqrt(jnp.sum(current[...] * current[...]))
    current[...] = current[...] / magnitude

    def put_split():
        for side in range(2):
            high, low = split(current[side])
            high_ref[:, side * half : (side + 1) * half] = high
            low_ref[:, side * half : (side + 1) * half] = low

    def cubic(high_rows, low_rows):
        gram = dot_t(high_rows, high_ref[...]) + (
            dot_t(high_rows, low_ref[...]) + dot_t(low_rows, high_ref[...])
        )
        high, low = split(gram)
        return dot(high, high_ref[...]) + (dot(high, low_ref[...]) + dot(low, high_ref[...]))

    def step(iteration, carry):
        put_split()
        update = cubic(high_ref[...], low_ref[...])
        for side in range(2):
            current[side] = 1.5 * current[side] - 0.5 * update[:, side * half : (side + 1) * half]
        return carry

    lax.fori_loop(0, NS_STEPS - 1, step, 0)
    put_split()
    rows = pl.ds(pl.multiple_of(own, 16), width)
    update = cubic(high_ref[rows, :], low_ref[rows, :])
    for side in range(2):
        rotation_out[:, side * half : (side + 1) * half] = (
            1.5 * current[side, rows, :] - 0.5 * update[:, side * half : (side + 1) * half]
        )

    sub_count, row_count = codes.shape
    rotated[:width, :] = dot(rotation_out[...].astype(jnp.bfloat16), vectors[...]).astype(jnp.bfloat16)
    rotated[width:, :] = jnp.ones((rotated.shape[0] - width, row_count), jnp.bfloat16)

    centroid_count = total.shape[0]
    row = lax.broadcasted_iota(jnp.int32, (centroid_count, row_count), 0)
    owner_rows = centroid_count // dp_count
    quarter_rows = centroid_count // 4
    position = row // quarter_rows
    inner = row % quarter_rows
    level = (((inner // owner_rows) ^ high_part) * 4 + (position ^ quarter)) * owner_rows + inner % owner_rows
    column = lax.broadcasted_iota(jnp.int32, total.shape, 1)
    subspace = jnp.where(column < width, column // sub_width, column - width)
    total[...] = jnp.zeros(total.shape, jnp.float32)
    for m in range(sub_count):
        onehot = (codes[m : m + 1, :] == level).astype(jnp.float32).astype(jnp.bfloat16)
        total[...] = jnp.where(subspace == m, dot_t(onehot, rotated[...]), total[...])
    for k, out in enumerate(outs):
        out[...] = total[k * quarter_rows : (k + 1) * quarter_rows, :]


def finish_kernel(sub_width, kept, received, out):
    total = kept[...] + received[...]
    width = out.shape[1]
    row = lax.broadcasted_iota(jnp.int32, (total.shape[1], width), 0)
    column = lax.broadcasted_iota(jnp.int32, (total.shape[1], width), 1)
    spread = (row == width + column // sub_width).astype(jnp.float32)
    counts = jnp.dot(total, spread, precision=lax.Precision.HIGHEST)
    out[...] = total[:, :width] / jnp.maximum(counts, 1.0)


def call(kernel, outs, scratch, *args):
    return pl.pallas_call(
        kernel,
        out_shape=[jax.ShapeDtypeStruct(s, jnp.float32) for s in outs],
        in_specs=[pl.BlockSpec(memory_space=pltpu.VMEM)] * len(args),
        out_specs=[pl.BlockSpec(memory_space=pltpu.VMEM)] * len(outs),
        scratch_shapes=scratch,
        compiler_params=pltpu.CompilerParams(vmem_limit_bytes=VMEM_LIMIT),
    )(*args)


def per_device(vectors, codes, codebook):
    width, row_count = vectors.shape
    sub_count = codes.shape[0]
    sub_width = width // sub_count
    centroid_count = codebook.shape[0]
    dp_count = lax.axis_size("dp")
    total_width = width * DIMS
    half, thin = 2 * width, width // 2
    high_masks = [4 << bit for bit in range(2, dp_count.bit_length() - 1)]

    book = codebook.T
    book_other, codes_other = swap(book, 2), swap(codes, 2)
    vectors_core = swap(vectors, 1)
    parts = call(
        functools.partial(cross_kernel, sub_width),
        [(thin, half)] * 4,
        [pltpu.VMEM((half, row_count), jnp.bfloat16), pltpu.VMEM((half, row_count), jnp.float32)],
        vectors, vectors_core, codes, codes_other, book, book_other,
    )
    held, vectors_late = lax.optimization_barrier((parts, vectors))
    vectors_pair = swap(vectors_late, 2)
    vectors_last = swap(vectors_pair, 1)

    piece = held[0] + swap(held[1], 4) + swap(held[2], 8) + swap(held[3], 12)
    for mask in high_masks:
        piece = piece + swap(piece, mask)
    pieces = [piece if mask == 0 else swap(piece, mask) for mask in range(0, 16, 2)]
    both = []
    for own in pieces:
        both += [own, swap(own, 1)]

    columns = width + sub_count
    columns += -columns % LANES
    rotation, *sums = call(
        functools.partial(refit_kernel, sub_width),
        [(width, total_width)] + [(centroid_count // 4, columns)] * 4,
        [
            pltpu.VMEM((2, total_width, half), jnp.float32),
            pltpu.VMEM((total_width, total_width), jnp.bfloat16),
            pltpu.VMEM((total_width, total_width), jnp.bfloat16),
            pltpu.VMEM((total_width, row_count), jnp.bfloat16),
            pltpu.VMEM((columns, row_count), jnp.bfloat16),
            pltpu.VMEM((centroid_count, columns), jnp.float32),
        ],
        *both, vectors, vectors_core, vectors_pair, vectors_last, codes,
    )
    held = sums[0] + swap(sums[1], 4) + swap(sums[2], 8) + swap(sums[3], 12)
    received = jnp.zeros_like(held)
    for step, mask in enumerate(reversed(high_masks)):
        if step:
            held = held + received
        middle = held.shape[0] // 2
        held, received = held[:middle], swap(held[middle:], mask)
    (new_codebook,) = call(
        functools.partial(finish_kernel, sub_width),
        [(centroid_count // dp_count, width)],
        [],
        held, received,
    )
    return rotation, new_codebook


def solution(mesh):
    placed = (P("dim", "dp"), P("dim", "dp"), P(None, "dim"))
    return jax.shard_map(
        per_device,
        mesh=mesh,
        in_specs=placed,
        out_specs=(P("dim", None), P("dp", "dim")),
        check_vma=False,
    )
```

```python
import functools

import jax
import jax.numpy as jnp
from jax import lax
from jax.experimental import pallas as pl
from jax.experimental.pallas import tpu as pltpu
from jax.sharding import PartitionSpec as P

NS_STEPS = 4
DIMS = 4
LANES = 128
VMEM_LIMIT = 56 * 1024 * 1024


def swap(value, mask):
    count = lax.axis_size("dp") * lax.axis_size("dim")
    return lax.ppermute(value, ("dp", "dim"), [(i, i ^ mask) for i in range(count)])


def place():
    dim = lax.axis_index("dim")
    dp = lax.axis_index("dp")
    return dim & 1, dim >> 1, dp & 3, dp >> 2


def split(value):
    high = value.astype(jnp.bfloat16)
    low = (value - high.astype(jnp.float32)).astype(jnp.bfloat16)
    return high, low


def dot_t(a, b):
    return lax.dot_general(a, b, (((1,), (1,)), ((), ())), preferred_element_type=jnp.float32)


def dot(a, b):
    return jnp.dot(a, b, preferred_element_type=jnp.float32)


def decode(codes_ref, book_ref, sub_width, write):
    sub_count, row_count = codes_ref.shape
    width = sub_count * sub_width
    sublane = lax.broadcasted_iota(jnp.int32, (8, row_count), 0)
    for first in range(0, width, 8):
        one, two = first // sub_width, (first + 7) // sub_width
        index = jnp.broadcast_to(codes_ref[one : one + 1, :], (8, row_count))
        if two != one:
            later = jnp.broadcast_to(codes_ref[two : two + 1, :], (8, row_count))
            index = jnp.where(sublane < two * sub_width - first, index, later)
        book = book_ref[first : first + 8, :].astype(jnp.float32)
        parts = []
        for start in range(0, row_count, LANES):
            at = index[:, start : start + LANES]
            inner = at & (LANES - 1)
            value = jnp.take_along_axis(book[:, :LANES], inner, axis=1, mode="promise_in_bounds")
            for level in range(LANES, book.shape[1], LANES):
                other = jnp.take_along_axis(
                    book[:, level : level + LANES], inner, axis=1, mode="promise_in_bounds"
                )
                value = jnp.where(at >= level, other, value)
            parts.append(value)
        write(first, jnp.concatenate(parts, axis=1))


def decoded_rows(codes, book, sub_width, rows):
    def write(row, value):
        rows[row : row + 8, :] = value

    decode(codes, book, sub_width, write)
    return rows[...].astype(jnp.bfloat16)


def own_cross_kernel(sub_width, v0, v1, codes, book, cross, vectors, rows):
    core, _, _, _ = place()
    width = v0.shape[0]
    for k, v in enumerate((v0, v1)):
        vectors[pl.ds(pl.multiple_of((core ^ k) * width, 16), width), :] = v[...]
    cross[...] = dot_t(decoded_rows(codes, book, sub_width, rows), vectors[...])


def other_cross_kernel(sub_width, vectors, own, codes, book, *rest):
    outs, (both, rows) = rest[:4], rest[4:]
    _, pair, quarter, _ = place()
    width = own.shape[0]
    thin = width // 2
    both[pl.ds(pl.multiple_of(pair * width, 8), width), :] = own[...]
    other = dot_t(decoded_rows(codes, book, sub_width, rows), vectors[...])
    both[pl.ds(pl.multiple_of((1 - pair) * width, 8), width), :] = other
    for k, out in enumerate(outs):
        out[...] = both[pl.ds(pl.multiple_of((quarter ^ k) * thin, 8), thin), :]


def gram_blocks(size, high, low, whole, write):
    count = high.shape[0] // size
    for i in range(count):
        a = pl.ds(i * size, size)
        for j in range(i, count):
            b = pl.ds(j * size, size)
            block = dot_t(high[a, :], high[b, :])
            if whole:
                block = block + (dot_t(high[a, :], low[b, :]) + dot_t(low[a, :], high[b, :]))
            block = block.astype(jnp.bfloat16)
            write(i, j, block)
            if i != j:
                write(j, i, block.T)


def refit_kernel(sub_width, *refs):
    pieces, sources, codes = refs[:16], refs[16:20], refs[20]
    rotation_out, outs = refs[21], refs[22:26]
    current, halves, gram, vectors, rotated, total, arrived = refs[26:]
    core, pair, quarter, high_part = place()
    dp_count = lax.axis_size("dp")
    thin, half = pieces[0].shape
    width, size = 2 * thin, current.shape[0]
    block = 2 * LANES
    own = (pair * 2 + core) * width

    copies = []
    for mask, piece in enumerate(pieces):
        c, p, q = core ^ (mask & 1), pair ^ (mask >> 1 & 1), quarter ^ (mask >> 2)
        row = ((q >> 1) * 2 + c) * width + (q & 1) * thin
        rows, columns = pl.ds(pl.multiple_of(row, 8), thin), pl.ds(pl.multiple_of(p * half, LANES), half)
        copies.append(pltpu.make_async_copy(piece, current.at[rows, columns], arrived.at[mask]))
    for k, source in enumerate(sources):
        at = ((pair ^ (k >> 1)) * 2 + (core ^ (k & 1))) * width
        rows = pl.ds(pl.multiple_of(at, 16), width)
        copies.append(pltpu.make_async_copy(source, vectors.at[rows, :], arrived.at[16 + k]))
    for copy in copies:
        copy.start()
    for copy in copies[:16]:
        copy.wait()
    squares = jnp.zeros((8, size), jnp.float32)
    for row in range(0, size, 8):
        value = current[row : row + 8, :]
        squares = squares + value * value
    magnitude = jnp.sqrt(jnp.sum(squares))
    for row in range(0, size, block):
        value = current[row : row + block, :] / magnitude
        current[row : row + block, :] = value
        halves[0, 0, row : row + block, :], halves[0, 1, row : row + block, :] = split(value)

    def step(iteration):
        now, later = iteration % 2, (iteration + 1) % 2
        high, low = halves.at[now, 0], halves.at[now, 1]

        def write(i, j, value):
            gram[pl.ds(i * block, block), pl.ds(j * block, block)] = value

        gram_blocks(block, high, low, iteration == 0, write)
        for row in range(0, size, block):
            rows = pl.ds(row, block)
            update = dot(gram[rows, :], high[...]) + dot(gram[rows, :], low[...])
            value = 1.5 * current[rows, :] - 0.5 * update
            current[rows, :] = value
            halves[later, 0, rows, :], halves[later, 1, rows, :] = split(value)

    for iteration in range(NS_STEPS - 1):
        step(iteration)
    last = (NS_STEPS - 1) % 2
    high, low = halves.at[last, 0], halves.at[last, 1]
    rows = pl.ds(pl.multiple_of(own, 16), width)
    own_gram = dot_t(high[rows, :], high[...]) + (
        dot_t(high[rows, :], low[...]) + dot_t(low[rows, :], high[...])
    )
    own_high, own_low = split(own_gram)
    update = dot(own_high, high[...]) + (dot(own_high, low[...]) + dot(own_low, high[...]))
    rotation = 1.5 * current[rows, :] - 0.5 * update
    rotation_out[...] = rotation

    for copy in copies[16:]:
        copy.wait()
    sub_count, row_count = codes.shape
    rotated[:width, :] = dot(rotation.astype(jnp.bfloat16), vectors[...]).astype(jnp.bfloat16)
    rotated[width:, :] = jnp.ones((rotated.shape[0] - width, row_count), jnp.bfloat16)

    centroid_count, columns = total.shape
    owner_rows = centroid_count // dp_count
    quarter_rows = centroid_count // 4
    row = lax.broadcasted_iota(jnp.int32, (centroid_count, LANES), 0)
    position = row // quarter_rows
    inner = row % quarter_rows
    level = (((inner // owner_rows) ^ high_part) * 4 + (position ^ quarter)) * owner_rows + inner % owner_rows
    level = jnp.concatenate([level] * (row_count // LANES), axis=1)
    column = lax.broadcasted_iota(jnp.int32, (8, columns), 1)
    subspace = jnp.where(column < width, column // sub_width, column - width)
    subspace = jnp.broadcast_to(subspace[:1], total.shape)
    for m in range(sub_count):
        onehot = (codes[m : m + 1, :] == level).astype(jnp.float32).astype(jnp.bfloat16)
        sums = dot_t(onehot, rotated[...])
        total[...] = jnp.where(subspace == m, sums, total[...] if m else 0.0)
    for k, out in enumerate(outs):
        out[...] = total[k * quarter_rows : (k + 1) * quarter_rows, :]


def finish_kernel(sub_width, kept, received, out):
    total = kept[...] + received[...]
    width = out.shape[1]
    row = lax.broadcasted_iota(jnp.int32, (total.shape[1], width), 0)
    column = lax.broadcasted_iota(jnp.int32, (total.shape[1], width), 1)
    spread = (row == width + column // sub_width).astype(jnp.float32)
    counts = jnp.dot(total, spread, precision=lax.Precision.HIGHEST)
    out[...] = total[:, :width] / jnp.maximum(counts, 1.0)


def floats(*shape):
    return jax.ShapeDtypeStruct(shape, jnp.float32)


def call(kernel, outs, scratch, far, *args):
    spaces = [pltpu.HBM] * far + [pltpu.VMEM] * (len(args) - far)
    return pl.pallas_call(
        kernel,
        out_shape=outs,
        in_specs=[pl.BlockSpec(memory_space=space) for space in spaces],
        out_specs=[pl.BlockSpec(memory_space=pltpu.VMEM)] * len(outs),
        scratch_shapes=scratch,
        compiler_params=pltpu.CompilerParams(vmem_limit_bytes=VMEM_LIMIT),
    )(*args)


def per_device(vectors, codes, codebook):
    width, row_count = vectors.shape
    sub_count = codes.shape[0]
    sub_width = width // sub_count
    centroid_count = codebook.shape[0]
    dp_count = lax.axis_size("dp")
    total_width = width * DIMS
    half, thin = 2 * width, width // 2
    high_masks = [4 << bit for bit in range(2, dp_count.bit_length() - 1)]

    book = codebook.T
    book_other, codes_other = swap(book, 2), swap(codes, 2)
    vectors_core = swap(vectors, 1)
    own_cross, own_vectors = call(
        functools.partial(own_cross_kernel, sub_width),
        [floats(width, half), jax.ShapeDtypeStruct((half, row_count), jnp.bfloat16)],
        [pltpu.VMEM((width, row_count), jnp.float32)],
        0,
        vectors, vectors_core, codes, book,
    )
    parts = call(
        functools.partial(other_cross_kernel, sub_width),
        [floats(thin, half)] * 4,
        [pltpu.VMEM((half, half), jnp.float32), pltpu.VMEM((width, row_count), jnp.float32)],
        0,
        own_vectors, own_cross, codes_other, book_other,
    )
    held, vectors_late = lax.optimization_barrier((parts, vectors))
    vectors_pair = swap(vectors_late, 2)
    vectors_last = swap(vectors_pair, 1)

    piece = held[0] + swap(held[1], 4) + swap(held[2], 8) + swap(held[3], 12)
    for mask in high_masks:
        piece = piece + swap(piece, mask)
    pieces = [piece if mask == 0 else swap(piece, mask) for mask in range(0, 16, 2)]
    both = []
    for own in pieces:
        both += [own, swap(own, 1)]

    columns = width + sub_count
    columns += -columns % LANES
    rotation, *sums = call(
        functools.partial(refit_kernel, sub_width),
        [floats(width, total_width)] + [floats(centroid_count // 4, columns)] * 4,
        [
            pltpu.VMEM((total_width, total_width), jnp.float32),
            pltpu.VMEM((2, 2, total_width, total_width), jnp.bfloat16),
            pltpu.VMEM((total_width, total_width), jnp.bfloat16),
            pltpu.VMEM((total_width, row_count), jnp.bfloat16),
            pltpu.VMEM((columns, row_count), jnp.bfloat16),
            pltpu.VMEM((centroid_count, columns), jnp.float32),
            pltpu.SemaphoreType.DMA((20,)),
        ],
        20,
        *both, vectors, vectors_core, vectors_pair, vectors_last, codes,
    )
    held = sums[0] + swap(sums[1], 4) + swap(sums[2], 8) + swap(sums[3], 12)
    received = jnp.zeros_like(held)
    for step, mask in enumerate(reversed(high_masks)):
        if step:
            held = held + received
        middle = held.shape[0] // 2
        held, received = held[:middle], swap(held[middle:], mask)
    (new_codebook,) = call(
        functools.partial(finish_kernel, sub_width),
        [floats(centroid_count // dp_count, width)],
        [],
        0,
        held, received,
    )
    return rotation, new_codebook


def solution(mesh):
    placed = (P("dim", "dp"), P("dim", "dp"), P(None, "dim"))
    return jax.shard_map(
        per_device,
        mesh=mesh,
        in_specs=placed,
        out_specs=(P("dim", None), P("dp", "dim")),
        check_vma=False,
    )
```

```python
import functools

import jax
import jax.numpy as jnp
from jax import lax
from jax.experimental import pallas as pl
from jax.experimental.pallas import tpu as pltpu
from jax.sharding import PartitionSpec as P

NS_STEPS = 4
DIMS = 4
LANES = 128
VMEM_LIMIT = 56 * 1024 * 1024


def swap(value, mask):
    count = lax.axis_size("dp") * lax.axis_size("dim")
    return lax.ppermute(value, ("dp", "dim"), [(i, i ^ mask) for i in range(count)])


def place():
    dim = lax.axis_index("dim")
    dp = lax.axis_index("dp")
    return dim & 1, dim >> 1, dp & 3, dp >> 2


def split(value):
    high = value.astype(jnp.bfloat16)
    low = (value - high.astype(jnp.float32)).astype(jnp.bfloat16)
    return high, low


def dot_t(a, b):
    return lax.dot_general(a, b, (((1,), (1,)), ((), ())), preferred_element_type=jnp.float32)


def dot(a, b):
    return jnp.dot(a, b, preferred_element_type=jnp.float32)


def decode(codes_ref, book_ref, sub_width, write):
    sub_count, row_count = codes_ref.shape
    width = sub_count * sub_width
    sublane = lax.broadcasted_iota(jnp.int32, (8, row_count), 0)
    for first in range(0, width, 8):
        one, two = first // sub_width, (first + 7) // sub_width
        index = jnp.broadcast_to(codes_ref[one : one + 1, :], (8, row_count))
        if two != one:
            later = jnp.broadcast_to(codes_ref[two : two + 1, :], (8, row_count))
            index = jnp.where(sublane < two * sub_width - first, index, later)
        book = book_ref[first : first + 8, :].astype(jnp.float32)
        parts = []
        for start in range(0, row_count, LANES):
            at = index[:, start : start + LANES]
            inner = at & (LANES - 1)
            value = jnp.take_along_axis(book[:, :LANES], inner, axis=1, mode="promise_in_bounds")
            for level in range(LANES, book.shape[1], LANES):
                other = jnp.take_along_axis(
                    book[:, level : level + LANES], inner, axis=1, mode="promise_in_bounds"
                )
                value = jnp.where(at >= level, other, value)
            parts.append(value)
        write(first, jnp.concatenate(parts, axis=1))


def decoded_rows(codes, book, sub_width, rows):
    def write(row, value):
        rows[row : row + 8, :] = value

    decode(codes, book, sub_width, write)
    return rows[...].astype(jnp.bfloat16)


def own_cross_kernel(sub_width, v0, v1, codes, book, cross, vectors, rows):
    core, _, _, _ = place()
    width = v0.shape[0]
    for k, v in enumerate((v0, v1)):
        vectors[pl.ds(pl.multiple_of((core ^ k) * width, 16), width), :] = v[...]
    cross[...] = dot_t(decoded_rows(codes, book, sub_width, rows), vectors[...])


def other_cross_kernel(sub_width, vectors, own, codes, book, *rest):
    outs, (both, rows) = rest[:4], rest[4:]
    _, pair, quarter, _ = place()
    width = own.shape[0]
    thin = width // 2
    both[pl.ds(pl.multiple_of(pair * width, 8), width), :] = own[...]
    other = dot_t(decoded_rows(codes, book, sub_width, rows), vectors[...])
    both[pl.ds(pl.multiple_of((1 - pair) * width, 8), width), :] = other
    for k, out in enumerate(outs):
        out[...] = both[pl.ds(pl.multiple_of((quarter ^ k) * thin, 8), thin), :]


def gram_blocks(size, high, low, whole, write):
    count = high.shape[0] // size
    for i in range(count):
        a = pl.ds(i * size, size)
        for j in range(i, count):
            b = pl.ds(j * size, size)
            block = dot_t(high[a, :], high[b, :])
            if whole:
                block = block + (dot_t(high[a, :], low[b, :]) + dot_t(low[a, :], high[b, :]))
            block = block.astype(jnp.bfloat16)
            write(i, j, block)
            if i != j:
                write(j, i, block.T)


def refit_kernel(sub_width, *refs):
    pieces, codes, sources = refs[:16], refs[16], refs[17:21]
    rotation_out, outs = refs[21], refs[22:26]
    current, halves, gram, vectors, rotated, total, arrived = refs[26:]
    core, pair, quarter, high_part = place()
    dp_count = lax.axis_size("dp")
    thin, half = pieces[0].shape
    width, size = 2 * thin, current.shape[0]
    block = 2 * LANES
    own = (pair * 2 + core) * width

    copies = []
    for k, source in enumerate(sources):
        at = ((pair ^ (k >> 1)) * 2 + (core ^ (k & 1))) * width
        rows = pl.ds(pl.multiple_of(at, 16), width)
        copies.append(pltpu.make_async_copy(source, vectors.at[rows, :], arrived.at[k]))
        copies[k].start()
    for mask, piece in enumerate(pieces):
        c, p, q = core ^ (mask & 1), pair ^ (mask >> 1 & 1), quarter ^ (mask >> 2)
        row = ((q >> 1) * 2 + c) * width + (q & 1) * thin
        rows, columns = pl.ds(pl.multiple_of(row, 8), thin), pl.ds(pl.multiple_of(p * half, LANES), half)
        current[rows, columns] = piece[...]
    squares = jnp.zeros((8, size), jnp.float32)
    for row in range(0, size, 8):
        value = current[row : row + 8, :]
        squares = squares + value * value
    magnitude = jnp.sqrt(jnp.sum(squares))
    for row in range(0, size, block):
        value = current[row : row + block, :] / magnitude
        current[row : row + block, :] = value
        halves[0, 0, row : row + block, :], halves[0, 1, row : row + block, :] = split(value)

    def step(iteration):
        now, later = iteration % 2, (iteration + 1) % 2
        high, low = halves.at[now, 0], halves.at[now, 1]

        def write(i, j, value):
            gram[pl.ds(i * block, block), pl.ds(j * block, block)] = value

        gram_blocks(block, high, low, iteration == 0, write)
        for row in range(0, size, block):
            rows = pl.ds(row, block)
            update = dot(gram[rows, :], high[...]) + dot(gram[rows, :], low[...])
            value = 1.5 * current[rows, :] - 0.5 * update
            current[rows, :] = value
            halves[later, 0, rows, :], halves[later, 1, rows, :] = split(value)

    for iteration in range(NS_STEPS - 1):
        step(iteration)
    last = (NS_STEPS - 1) % 2
    high, low = halves.at[last, 0], halves.at[last, 1]
    rows = pl.ds(pl.multiple_of(own, 16), width)
    own_gram = dot_t(high[rows, :], high[...]) + (
        dot_t(high[rows, :], low[...]) + dot_t(low[rows, :], high[...])
    )
    own_high, own_low = split(own_gram)
    update = dot(own_high, high[...]) + (dot(own_high, low[...]) + dot(own_low, high[...]))
    rotation = 1.5 * current[rows, :] - 0.5 * update
    rotation_out[...] = rotation

    for copy in copies:
        copy.wait()
    sub_count, row_count = codes.shape
    rotated[:width, :] = dot(rotation.astype(jnp.bfloat16), vectors[...]).astype(jnp.bfloat16)
    rotated[width:, :] = jnp.ones((rotated.shape[0] - width, row_count), jnp.bfloat16)

    centroid_count, columns = total.shape
    owner_rows = centroid_count // dp_count
    quarter_rows = centroid_count // 4
    row = lax.broadcasted_iota(jnp.int32, (centroid_count, LANES), 0)
    position = row // quarter_rows
    inner = row % quarter_rows
    level = (((inner // owner_rows) ^ high_part) * 4 + (position ^ quarter)) * owner_rows + inner % owner_rows
    level = jnp.concatenate([level] * (row_count // LANES), axis=1)
    column = lax.broadcasted_iota(jnp.int32, (8, columns), 1)
    subspace = jnp.where(column < width, column // sub_width, column - width)
    subspace = jnp.broadcast_to(subspace[:1], total.shape)
    for m in range(sub_count):
        onehot = (codes[m : m + 1, :] == level).astype(jnp.float32).astype(jnp.bfloat16)
        sums = dot_t(onehot, rotated[...])
        total[...] = jnp.where(subspace == m, sums, total[...] if m else 0.0)
    for k, out in enumerate(outs):
        out[...] = total[k * quarter_rows : (k + 1) * quarter_rows, :]


def finish_kernel(sub_width, kept, received, out):
    total = kept[...] + received[...]
    width = out.shape[1]
    row = lax.broadcasted_iota(jnp.int32, (total.shape[1], width), 0)
    column = lax.broadcasted_iota(jnp.int32, (total.shape[1], width), 1)
    spread = (row == width + column // sub_width).astype(jnp.float32)
    counts = jnp.dot(total, spread, precision=lax.Precision.HIGHEST)
    out[...] = total[:, :width] / jnp.maximum(counts, 1.0)


def floats(*shape):
    return jax.ShapeDtypeStruct(shape, jnp.float32)


def near(value):
    return pltpu.with_memory_space_constraint(value, pltpu.VMEM)


def call(kernel, outs, scratch, far, *args):
    spaces = [pltpu.VMEM] * (len(args) - far) + [pl.ANY] * far
    return pl.pallas_call(
        kernel,
        out_shape=outs,
        in_specs=[pl.BlockSpec(memory_space=space) for space in spaces],
        out_specs=[pl.BlockSpec(memory_space=pltpu.VMEM)] * len(outs),
        scratch_shapes=scratch,
        compiler_params=pltpu.CompilerParams(vmem_limit_bytes=VMEM_LIMIT),
    )(*args)


def per_device(vectors, codes, codebook):
    width, row_count = vectors.shape
    sub_count = codes.shape[0]
    sub_width = width // sub_count
    centroid_count = codebook.shape[0]
    dp_count = lax.axis_size("dp")
    total_width = width * DIMS
    half, thin = 2 * width, width // 2
    high_masks = [4 << bit for bit in range(2, dp_count.bit_length() - 1)]

    book = codebook.T
    book_other, codes_other = swap(book, 2), swap(codes, 2)
    vectors_core = swap(vectors, 1)
    own_cross, own_vectors = call(
        functools.partial(own_cross_kernel, sub_width),
        [pltpu.VMEM((width, half), jnp.float32), pltpu.VMEM((half, row_count), jnp.bfloat16)],
        [pltpu.VMEM((width, row_count), jnp.float32)],
        0,
        vectors, near(vectors_core), codes, book,
    )
    parts = call(
        functools.partial(other_cross_kernel, sub_width),
        [pltpu.VMEM((thin, half), jnp.float32)] * 4,
        [pltpu.VMEM((half, half), jnp.float32), pltpu.VMEM((width, row_count), jnp.float32)],
        0,
        near(own_vectors), near(own_cross), near(codes_other), near(book_other),
    )
    held, vectors_late = lax.optimization_barrier((parts, vectors))
    vectors_pair = swap(vectors_late, 2)
    vectors_last = swap(vectors_pair, 1)

    piece = held[0] + swap(held[1], 4) + swap(held[2], 8) + swap(held[3], 12)
    for mask in high_masks:
        piece = piece + swap(piece, mask)
    pieces = [piece if mask == 0 else swap(piece, mask) for mask in range(0, 16, 2)]
    both = []
    for own in pieces:
        both += [own, swap(own, 1)]

    columns = width + sub_count
    columns += -columns % LANES
    rotation, *sums = call(
        functools.partial(refit_kernel, sub_width),
        [floats(width, total_width)] + [pltpu.VMEM((centroid_count // 4, columns), jnp.float32)] * 4,
        [
            pltpu.VMEM((total_width, total_width), jnp.float32),
            pltpu.VMEM((2, 2, total_width, total_width), jnp.bfloat16),
            pltpu.VMEM((total_width, total_width), jnp.bfloat16),
            pltpu.VMEM((total_width, row_count), jnp.bfloat16),
            pltpu.VMEM((columns, row_count), jnp.bfloat16),
            pltpu.VMEM((centroid_count, columns), jnp.float32),
            pltpu.SemaphoreType.DMA((4,)),
        ],
        4,
        *map(near, both), codes, vectors, near(vectors_core), near(vectors_pair), near(vectors_last),
    )
    held = sums[0] + swap(sums[1], 4) + swap(sums[2], 8) + swap(sums[3], 12)
    received = jnp.zeros_like(held)
    for step, mask in enumerate(reversed(high_masks)):
        if step:
            held = held + received
        middle = held.shape[0] // 2
        held, received = held[:middle], swap(held[middle:], mask)
    (new_codebook,) = call(
        functools.partial(finish_kernel, sub_width),
        [floats(centroid_count // dp_count, width)],
        [],
        0,
        near(held), near(received),
    )
    return rotation, new_codebook


def solution(mesh):
    placed = (P("dim", "dp"), P("dim", "dp"), P(None, "dim"))
    return jax.shard_map(
        per_device,
        mesh=mesh,
        in_specs=placed,
        out_specs=(P("dim", None), P("dp", "dim")),
        check_vma=False,
    )
```

```python
import functools

import jax
import jax.numpy as jnp
from jax import lax
from jax.experimental import pallas as pl
from jax.experimental.pallas import tpu as pltpu
from jax.sharding import PartitionSpec as P

NS_STEPS = 4
DIMS = 4
LANES = 128
TAIL = 16
TINY = 1e-30
ROUNDS = ((4, 8), (2, 12), (10, 6))
LAST = 14
VMEM_LIMIT = 56 * 1024 * 1024


def swap(value, mask):
    count = lax.axis_size("dp") * lax.axis_size("dim")
    return lax.ppermute(value, ("dp", "dim"), [(i, i ^ mask) for i in range(count)])


def swap_by_core(value, one, two):
    count = lax.axis_size("dp") * lax.axis_size("dim")
    return lax.ppermute(value, ("dp", "dim"), [(i, i ^ (two if i & 1 else one)) for i in range(count)])


def place():
    dim = lax.axis_index("dim")
    dp = lax.axis_index("dp")
    return dim & 1, dim >> 1, dp & 3, dp >> 2


def split(value):
    high = value.astype(jnp.bfloat16)
    low = (value - high.astype(jnp.float32)).astype(jnp.bfloat16)
    return high, low


def dot_t(a, b):
    return lax.dot_general(a, b, (((1,), (1,)), ((), ())), preferred_element_type=jnp.float32)


def dot(a, b):
    return jnp.dot(a, b, preferred_element_type=jnp.float32)


def decode(codes_ref, book_ref, sub_width, write):
    sub_count, row_count = codes_ref.shape
    width = sub_count * sub_width
    sublane = lax.broadcasted_iota(jnp.int32, (8, row_count), 0)
    for first in range(0, width, 8):
        one, two = first // sub_width, (first + 7) // sub_width
        index = jnp.broadcast_to(codes_ref[one : one + 1, :], (8, row_count))
        if two != one:
            later = jnp.broadcast_to(codes_ref[two : two + 1, :], (8, row_count))
            index = jnp.where(sublane < two * sub_width - first, index, later)
        book = book_ref[first : first + 8, :].astype(jnp.float32)
        parts = []
        for start in range(0, row_count, LANES):
            at = index[:, start : start + LANES]
            inner = at & (LANES - 1)
            value = jnp.take_along_axis(book[:, :LANES], inner, axis=1, mode="promise_in_bounds")
            for level in range(LANES, book.shape[1], LANES):
                other = jnp.take_along_axis(
                    book[:, level : level + LANES], inner, axis=1, mode="promise_in_bounds"
                )
                value = jnp.where(at >= level, other, value)
            parts.append(value)
        write(first, jnp.concatenate(parts, axis=1))


def decoded_rows(codes, book, sub_width, rows):
    def write(row, value):
        rows[row : row + 8, :] = value

    decode(codes, book, sub_width, write)
    return rows[...].astype(jnp.bfloat16)


def own_cross_kernel(sub_width, v0, v1, codes, book, cross, vectors, rows):
    core, _, _, _ = place()
    width = v0.shape[0]
    for k, v in enumerate((v0, v1)):
        vectors[pl.ds(pl.multiple_of((core ^ k) * width, 16), width), :] = v[...]
    cross[...] = dot_t(decoded_rows(codes, book, sub_width, rows), vectors[...])


def other_cross_kernel(sub_width, vectors, own, codes, book, *rest):
    outs, (both, rows) = rest[:4], rest[4:]
    _, pair, quarter, _ = place()
    width = own.shape[0]
    thin = width // 2
    both[pl.ds(pl.multiple_of(pair * width, 8), width), :] = own[...]
    other = dot_t(decoded_rows(codes, book, sub_width, rows), vectors[...])
    both[pl.ds(pl.multiple_of((1 - pair) * width, 8), width), :] = other
    for k, out in enumerate(outs):
        out[...] = both[pl.ds(pl.multiple_of((quarter ^ k) * thin, 8), thin), :]


def code_kernel(kept, received, kept_other, received_other, both, mine):
    core, _, _, _ = place()
    count = kept.shape[0]
    for k, (one, two) in enumerate(((kept, received), (kept_other, received_other))):
        total = one[...] + two[...]
        top = jnp.maximum(jnp.max(jnp.abs(total), axis=0, keepdims=True), TINY)
        exponent = jnp.ceil(jnp.log2(top))
        scaled = jnp.round(total * jnp.exp2(15.0 - exponent))
        coded = jnp.clip(scaled, -32767.0, 32767.0).astype(jnp.int32).astype(jnp.int16)
        tail = jnp.broadcast_to(exponent, (TAIL, total.shape[1])).astype(jnp.int32).astype(jnp.int16)
        first = pl.multiple_of((core ^ k) * (count + TAIL), TAIL)
        both[pl.ds(first, count), :] = coded
        both[pl.ds(pl.multiple_of(first + count, TAIL), TAIL), :] = tail
        if k == 0:
            mine[:count, :] = coded
            mine[count:, :] = tail


def decoded_piece(ref, first, count):
    exponent = ref[first + count : first + count + TAIL, :].astype(jnp.int32).astype(jnp.float32)[:1]
    coded = ref[first : first + count, :].astype(jnp.int32).astype(jnp.float32)
    return coded * jnp.exp2(exponent - 15.0)


def gram_blocks(size, high, low, whole, write):
    count = high.shape[0] // size
    for i in range(count):
        a = pl.ds(i * size, size)
        for j in range(i, count):
            b = pl.ds(j * size, size)
            block = dot_t(high[a, :], high[b, :])
            if whole:
                block = block + (dot_t(high[a, :], low[b, :]) + dot_t(low[a, :], high[b, :]))
            block = block.astype(jnp.bfloat16)
            write(i, j, block)
            if i != j:
                write(j, i, block.T)


def refit_kernel(sub_width, *refs):
    pairs, singles, codes, sources = refs[:7], refs[7:9], refs[9], refs[10:14]
    rotation_out, outs = refs[14], refs[15:19]
    current, halves, gram, vectors, rotated, total, arrived = refs[19:]
    core, pair, quarter, high_part = place()
    dp_count = lax.axis_size("dp")
    thin, half = singles[0].shape[0] - TAIL, singles[0].shape[1]
    width, size = 2 * thin, current.shape[0]
    block = 2 * LANES
    own = (pair * 2 + core) * width

    copies = []
    for k, source in enumerate(sources):
        at = ((pair ^ (k >> 1)) * 2 + (core ^ (k & 1))) * width
        rows = pl.ds(pl.multiple_of(at, 16), width)
        copies.append(pltpu.make_async_copy(source, vectors.at[rows, :], arrived.at[k]))
        copies[k].start()

    def place_piece(mask, c, ref, first):
        p, q = pair ^ (mask >> 1 & 1), quarter ^ (mask >> 2)
        row = ((q >> 1) * 2 + c) * width + (q & 1) * thin
        rows, columns = pl.ds(pl.multiple_of(row, 8), thin), pl.ds(pl.multiple_of(p * half, LANES), half)
        current[rows, columns] = decoded_piece(ref, first, thin)

    masks = [0] + [jnp.where(core == c, one, two) for c in (0, 1) for one, two in ROUNDS]
    for mask, ref in zip(masks, pairs):
        for c in (0, 1):
            place_piece(mask, c, ref, c * (thin + TAIL))
    for k, ref in enumerate(singles):
        place_piece(LAST, core ^ k, ref, 0)
    squares = jnp.zeros((8, size), jnp.float32)
    for row in range(0, size, 8):
        value = current[row : row + 8, :]
        squares = squares + value * value
    magnitude = jnp.sqrt(jnp.sum(squares))
    for row in range(0, size, block):
        value = current[row : row + block, :] / magnitude
        current[row : row + block, :] = value
        halves[0, 0, row : row + block, :], halves[0, 1, row : row + block, :] = split(value)

    def step(iteration):
        now, later = iteration % 2, (iteration + 1) % 2
        high, low = halves.at[now, 0], halves.at[now, 1]

        def write(i, j, value):
            gram[pl.ds(i * block, block), pl.ds(j * block, block)] = value

        gram_blocks(block, high, low, iteration == 0, write)
        for row in range(0, size, block):
            rows = pl.ds(row, block)
            update = dot(gram[rows, :], high[...]) + dot(gram[rows, :], low[...])
            value = 1.5 * current[rows, :] - 0.5 * update
            current[rows, :] = value
            halves[later, 0, rows, :], halves[later, 1, rows, :] = split(value)

    for iteration in range(NS_STEPS - 1):
        step(iteration)
    last = (NS_STEPS - 1) % 2
    high, low = halves.at[last, 0], halves.at[last, 1]
    rows = pl.ds(pl.multiple_of(own, 16), width)
    own_gram = dot_t(high[rows, :], high[...]) + (
        dot_t(high[rows, :], low[...]) + dot_t(low[rows, :], high[...])
    )
    own_high, own_low = split(own_gram)
    update = dot(own_high, high[...]) + (dot(own_high, low[...]) + dot(own_low, high[...]))
    rotation = 1.5 * current[rows, :] - 0.5 * update
    rotation_out[...] = rotation

    for copy in copies:
        copy.wait()
    sub_count, row_count = codes.shape
    rotated[:width, :] = dot(rotation.astype(jnp.bfloat16), vectors[...]).astype(jnp.bfloat16)
    rotated[width:, :] = jnp.ones((rotated.shape[0] - width, row_count), jnp.bfloat16)

    centroid_count, columns = total.shape
    owner_rows = centroid_count // dp_count
    quarter_rows = centroid_count // 4
    row = lax.broadcasted_iota(jnp.int32, (centroid_count, LANES), 0)
    position = row // quarter_rows
    inner = row % quarter_rows
    level = (((inner // owner_rows) ^ high_part) * 4 + (position ^ quarter)) * owner_rows + inner % owner_rows
    level = jnp.concatenate([level] * (row_count // LANES), axis=1)
    column = lax.broadcasted_iota(jnp.int32, (8, columns), 1)
    subspace = jnp.where(column < width, column // sub_width, column - width)
    subspace = jnp.broadcast_to(subspace[:1], total.shape)
    for m in range(sub_count):
        onehot = (codes[m : m + 1, :] == level).astype(jnp.float32).astype(jnp.bfloat16)
        sums = dot_t(onehot, rotated[...])
        total[...] = jnp.where(subspace == m, sums, total[...] if m else 0.0)
    for k, out in enumerate(outs):
        out[...] = total[k * quarter_rows : (k + 1) * quarter_rows, :]


def finish_kernel(sub_width, kept, received, out):
    total = kept[...] + received[...]
    width = out.shape[1]
    row = lax.broadcasted_iota(jnp.int32, (total.shape[1], width), 0)
    column = lax.broadcasted_iota(jnp.int32, (total.shape[1], width), 1)
    spread = (row == width + column // sub_width).astype(jnp.float32)
    counts = jnp.dot(total, spread, precision=lax.Precision.HIGHEST)
    out[...] = total[:, :width] / jnp.maximum(counts, 1.0)


def floats(*shape):
    return jax.ShapeDtypeStruct(shape, jnp.float32)


def near(value):
    return pltpu.with_memory_space_constraint(value, pltpu.VMEM)


def call(kernel, outs, scratch, far, *args):
    spaces = [pltpu.VMEM] * (len(args) - far) + [pl.ANY] * far
    return pl.pallas_call(
        kernel,
        out_shape=outs,
        in_specs=[pl.BlockSpec(memory_space=space) for space in spaces],
        out_specs=[pl.BlockSpec(memory_space=pltpu.VMEM)] * len(outs),
        scratch_shapes=scratch,
        compiler_params=pltpu.CompilerParams(vmem_limit_bytes=VMEM_LIMIT),
    )(*args)


def per_device(vectors, codes, codebook):
    width, row_count = vectors.shape
    sub_count = codes.shape[0]
    sub_width = width // sub_count
    centroid_count = codebook.shape[0]
    dp_count = lax.axis_size("dp")
    total_width = width * DIMS
    half, thin = 2 * width, width // 2
    high_masks = [4 << bit for bit in range(2, dp_count.bit_length() - 1)]

    book = codebook.T
    book_other, codes_other = swap(book, 2), swap(codes, 2)
    vectors_core = swap(vectors, 1)
    own_cross, own_vectors = call(
        functools.partial(own_cross_kernel, sub_width),
        [pltpu.VMEM((width, half), jnp.float32), pltpu.VMEM((half, row_count), jnp.bfloat16)],
        [pltpu.VMEM((width, row_count), jnp.float32)],
        0,
        vectors, near(vectors_core), codes, book,
    )
    parts = call(
        functools.partial(other_cross_kernel, sub_width),
        [pltpu.VMEM((thin, half), jnp.float32)] * 4,
        [pltpu.VMEM((half, half), jnp.float32), pltpu.VMEM((width, row_count), jnp.float32)],
        0,
        near(own_vectors), near(own_cross), near(codes_other), near(book_other),
    )
    held, vectors_late = lax.optimization_barrier((parts, vectors))
    vectors_pair = swap(vectors_late, 2)
    vectors_last = swap(vectors_pair, 1)

    piece = held[0] + swap(held[1], 4) + swap(held[2], 8) + swap(held[3], 12)
    for mask in high_masks[:-1]:
        piece = piece + swap(piece, mask)
    received = swap(piece, high_masks[-1])
    own_pair, own_piece = call(
        code_kernel,
        [pltpu.VMEM((2 * (thin + TAIL), half), jnp.int16), pltpu.VMEM((thin + TAIL, half), jnp.int16)],
        [],
        0,
        *map(near, (piece, received, swap(piece, 1), swap(received, 1))),
    )
    pairs = [swap_by_core(own_pair, one, two) for one, two in ROUNDS]
    last = swap(own_piece, LAST)
    gathered = [own_pair, *pairs, *(swap(pair, 1) for pair in pairs), last, swap(last, 1)]

    columns = width + sub_count
    columns += -columns % LANES
    rotation, *sums = call(
        functools.partial(refit_kernel, sub_width),
        [floats(width, total_width)] + [pltpu.VMEM((centroid_count // 4, columns), jnp.float32)] * 4,
        [
            pltpu.VMEM((total_width, total_width), jnp.float32),
            pltpu.VMEM((2, 2, total_width, total_width), jnp.bfloat16),
            pltpu.VMEM((total_width, total_width), jnp.bfloat16),
            pltpu.VMEM((total_width, row_count), jnp.bfloat16),
            pltpu.VMEM((columns, row_count), jnp.bfloat16),
            pltpu.VMEM((centroid_count, columns), jnp.float32),
            pltpu.SemaphoreType.DMA((4,)),
        ],
        4,
        *map(near, gathered), codes, vectors, near(vectors_core), near(vectors_pair), near(vectors_last),
    )
    held = sums[0] + swap(sums[1], 4) + swap(sums[2], 8) + swap(sums[3], 12)
    received = jnp.zeros_like(held)
    for step, mask in enumerate(reversed(high_masks)):
        if step:
            held = held + received
        middle = held.shape[0] // 2
        held, received = held[:middle], swap(held[middle:], mask)
    (new_codebook,) = call(
        functools.partial(finish_kernel, sub_width),
        [floats(centroid_count // dp_count, width)],
        [],
        0,
        near(held), near(received),
    )
    return rotation, new_codebook


def solution(mesh):
    placed = (P("dim", "dp"), P("dim", "dp"), P(None, "dim"))
    return jax.shard_map(
        per_device,
        mesh=mesh,
        in_specs=placed,
        out_specs=(P("dim", None), P("dp", "dim")),
        check_vma=False,
    )
```

```python
import functools

import jax
import jax.numpy as jnp
from jax import lax
from jax.experimental import pallas as pl
from jax.experimental.pallas import tpu as pltpu
from jax.sharding import PartitionSpec as P

NS_STEPS = 4
DIMS = 4
LANES = 128
TAIL = 16
TINY = 1e-30
ROUNDS = ((4, 8), (2, 12), (10, 6))
LAST = 14
VMEM_LIMIT = 56 * 1024 * 1024


def swap(value, mask):
    count = lax.axis_size("dp") * lax.axis_size("dim")
    return lax.ppermute(value, ("dp", "dim"), [(i, i ^ mask) for i in range(count)])


def swap_by_core(value, one, two):
    count = lax.axis_size("dp") * lax.axis_size("dim")
    return lax.ppermute(value, ("dp", "dim"), [(i, i ^ (two if i & 1 else one)) for i in range(count)])


def place():
    dim = lax.axis_index("dim")
    dp = lax.axis_index("dp")
    return dim & 1, dim >> 1, dp & 3, dp >> 2


def split(value):
    high = value.astype(jnp.bfloat16)
    low = (value - high.astype(jnp.float32)).astype(jnp.bfloat16)
    return high, low


def dot_t(a, b):
    return lax.dot_general(a, b, (((1,), (1,)), ((), ())), preferred_element_type=jnp.float32)


def dot(a, b):
    return jnp.dot(a, b, preferred_element_type=jnp.float32)


def decode(codes_ref, book_ref, sub_width, write):
    sub_count, row_count = codes_ref.shape
    codes = codes_ref[...].astype(jnp.int32)
    width = sub_count * sub_width
    sublane = lax.broadcasted_iota(jnp.int32, (8, row_count), 0)
    for first in range(0, width, 8):
        one, two = first // sub_width, (first + 7) // sub_width
        index = jnp.broadcast_to(codes[one : one + 1, :], (8, row_count))
        if two != one:
            later = jnp.broadcast_to(codes[two : two + 1, :], (8, row_count))
            index = jnp.where(sublane < two * sub_width - first, index, later)
        book = book_ref[first : first + 8, :].astype(jnp.float32)
        parts = []
        for start in range(0, row_count, LANES):
            at = index[:, start : start + LANES]
            inner = at & (LANES - 1)
            value = jnp.take_along_axis(book[:, :LANES], inner, axis=1, mode="promise_in_bounds")
            for level in range(LANES, book.shape[1], LANES):
                other = jnp.take_along_axis(
                    book[:, level : level + LANES], inner, axis=1, mode="promise_in_bounds"
                )
                value = jnp.where(at >= level, other, value)
            parts.append(value)
        write(first, jnp.concatenate(parts, axis=1))


def decoded_rows(codes, book, sub_width, rows):
    def write(row, value):
        rows[row : row + 8, :] = value

    decode(codes, book, sub_width, write)
    return rows[...].astype(jnp.bfloat16)


def own_cross_kernel(sub_width, v0, v1, codes, book, cross, vectors, rows):
    core, _, _, _ = place()
    width = v0.shape[0]
    for k, v in enumerate((v0, v1)):
        vectors[pl.ds(pl.multiple_of((core ^ k) * width, 16), width), :] = v[...]
    cross[...] = dot_t(decoded_rows(codes, book, sub_width, rows), vectors[...])


def other_cross_kernel(sub_width, vectors, own, codes, book, *rest):
    outs, (both, rows) = rest[:4], rest[4:]
    _, pair, quarter, _ = place()
    width = own.shape[0]
    thin = width // 2
    both[pl.ds(pl.multiple_of(pair * width, 8), width), :] = own[...]
    other = dot_t(decoded_rows(codes, book, sub_width, rows), vectors[...])
    both[pl.ds(pl.multiple_of((1 - pair) * width, 8), width), :] = other
    for k, out in enumerate(outs):
        out[...] = both[pl.ds(pl.multiple_of((quarter ^ k) * thin, 8), thin), :]


def code_kernel(kept, received, kept_other, received_other, both, mine):
    core, _, _, _ = place()
    count = kept.shape[0]
    exponents = []
    for k, (one, two) in enumerate(((kept, received), (kept_other, received_other))):
        total = one[...] + two[...]
        top = jnp.maximum(jnp.max(jnp.abs(total), axis=0, keepdims=True), TINY)
        exponent = jnp.ceil(jnp.log2(top))
        scaled = jnp.round(total * jnp.exp2(15.0 - exponent))
        coded = jnp.clip(scaled, -32767.0, 32767.0).astype(jnp.int32).astype(jnp.int16)
        exponents.append(jnp.broadcast_to(exponent, (TAIL, total.shape[1])).astype(jnp.int32))
        both[pl.ds(pl.multiple_of((core ^ k) * count, TAIL), count), :] = coded
        if k == 0:
            mine[:count, :] = coded
    row = lax.broadcasted_iota(jnp.int32, exponents[0].shape, 0)
    both[2 * count :, :] = jnp.where((row < TAIL // 2) == (core == 0), *exponents).astype(jnp.int16)
    mine[count:, :] = exponents[0].astype(jnp.int16)


def decoded_piece(ref, first, count, half):
    tail = ref[ref.shape[0] - TAIL :, :].astype(jnp.int32).astype(jnp.float32)
    exponent = tail[half * (TAIL // 2) : half * (TAIL // 2) + 1]
    coded = ref[first : first + count, :].astype(jnp.int32).astype(jnp.float32)
    return coded * jnp.exp2(exponent - 15.0)


def gram_blocks(size, high, low, whole, write):
    count = high.shape[0] // size
    for i in range(count):
        a = pl.ds(i * size, size)
        for j in range(i, count):
            b = pl.ds(j * size, size)
            block = dot_t(high[a, :], high[b, :])
            if whole:
                block = block + (dot_t(high[a, :], low[b, :]) + dot_t(low[a, :], high[b, :]))
            block = block.astype(jnp.bfloat16)
            write(i, j, block)
            if i != j:
                write(j, i, block.T)


def refit_kernel(sub_width, *refs):
    pairs, singles, codes, sources = refs[:7], refs[7:9], refs[9], refs[10:14]
    rotation_out, outs = refs[14], refs[15:19]
    current, halves, gram, vectors, rotated, total, arrived = refs[19:]
    core, pair, quarter, high_part = place()
    dp_count = lax.axis_size("dp")
    thin, half = singles[0].shape[0] - TAIL, singles[0].shape[1]
    width, size = 2 * thin, current.shape[0]
    block = 2 * LANES
    own = (pair * 2 + core) * width

    copies = []
    for k, source in enumerate(sources):
        at = ((pair ^ (k >> 1)) * 2 + (core ^ (k & 1))) * width
        rows = pl.ds(pl.multiple_of(at, 16), width)
        copies.append(pltpu.make_async_copy(source, vectors.at[rows, :], arrived.at[k]))
        copies[k].start()

    def place_piece(mask, c, ref, part):
        p, q = pair ^ (mask >> 1 & 1), quarter ^ (mask >> 2)
        row = ((q >> 1) * 2 + c) * width + (q & 1) * thin
        rows, columns = pl.ds(pl.multiple_of(row, 8), thin), pl.ds(pl.multiple_of(p * half, LANES), half)
        current[rows, columns] = decoded_piece(ref, part * thin, thin, part)

    masks = [0] + [jnp.where(core == c, one, two) for c in (0, 1) for one, two in ROUNDS]
    for mask, ref in zip(masks, pairs):
        for c in (0, 1):
            place_piece(mask, c, ref, c)
    for k, ref in enumerate(singles):
        place_piece(LAST, core ^ k, ref, 0)
    squares = jnp.zeros((8, size), jnp.float32)
    for row in range(0, size, 8):
        value = current[row : row + 8, :]
        squares = squares + value * value
    magnitude = jnp.sqrt(jnp.sum(squares))
    for row in range(0, size, block):
        value = current[row : row + block, :] / magnitude
        current[row : row + block, :] = value
        halves[0, 0, row : row + block, :], halves[0, 1, row : row + block, :] = split(value)

    def step(iteration):
        now, later = iteration % 2, (iteration + 1) % 2
        high, low = halves.at[now, 0], halves.at[now, 1]

        def write(i, j, value):
            gram[pl.ds(i * block, block), pl.ds(j * block, block)] = value

        gram_blocks(block, high, low, iteration == 0, write)
        for row in range(0, size, block):
            rows = pl.ds(row, block)
            update = dot(gram[rows, :], high[...]) + dot(gram[rows, :], low[...])
            value = 1.5 * current[rows, :] - 0.5 * update
            current[rows, :] = value
            halves[later, 0, rows, :], halves[later, 1, rows, :] = split(value)

    for iteration in range(NS_STEPS - 1):
        step(iteration)
    last = (NS_STEPS - 1) % 2
    high, low = halves.at[last, 0], halves.at[last, 1]
    rows = pl.ds(pl.multiple_of(own, 16), width)
    stacked = halves.at[(NS_STEPS - 2) % 2, 0]

    def thin_product(product, a_high, a_low):
        stacked[:width, :], stacked[width : 2 * width, :] = a_high, a_low
        with_high = product(stacked[: 2 * width, :], high[...])
        return with_high[:width] + (with_high[width:] + product(stacked[:width, :], low[...]))

    own_gram = thin_product(dot_t, high[rows, :], low[rows, :])
    update = thin_product(dot, *split(own_gram))
    rotation = 1.5 * current[rows, :] - 0.5 * update
    rotation_out[...] = rotation

    for copy in copies:
        copy.wait()
    sub_count, row_count = codes.shape
    rotated[:width, :] = dot(rotation.astype(jnp.bfloat16), vectors[...]).astype(jnp.bfloat16)
    rotated[width:, :] = jnp.ones((rotated.shape[0] - width, row_count), jnp.bfloat16)

    centroid_count, columns = total.shape
    owner_rows = centroid_count // dp_count
    quarter_rows = centroid_count // 4
    row = lax.broadcasted_iota(jnp.int32, (centroid_count, LANES), 0)
    position = row // quarter_rows
    inner = row % quarter_rows
    level = (((inner // owner_rows) ^ high_part) * 4 + (position ^ quarter)) * owner_rows + inner % owner_rows
    level = jnp.concatenate([level] * (row_count // LANES), axis=1)
    column = lax.broadcasted_iota(jnp.int32, (8, columns), 1)
    subspace = jnp.where(column < width, column // sub_width, column - width)
    subspace = jnp.broadcast_to(subspace[:1], total.shape)
    for m in range(sub_count):
        onehot = (codes[m : m + 1, :] == level).astype(jnp.float32).astype(jnp.bfloat16)
        sums = dot_t(onehot, rotated[...])
        total[...] = jnp.where(subspace == m, sums, total[...] if m else 0.0)
    for k, out in enumerate(outs):
        out[...] = total[k * quarter_rows : (k + 1) * quarter_rows, :]


def finish_kernel(sub_width, kept, received, out):
    total = kept[...] + received[...]
    width = out.shape[1]
    row = lax.broadcasted_iota(jnp.int32, (total.shape[1], width), 0)
    column = lax.broadcasted_iota(jnp.int32, (total.shape[1], width), 1)
    spread = (row == width + column // sub_width).astype(jnp.float32)
    counts = jnp.dot(total, spread, precision=lax.Precision.HIGHEST)
    out[...] = total[:, :width] / jnp.maximum(counts, 1.0)


def floats(*shape):
    return jax.ShapeDtypeStruct(shape, jnp.float32)


def near(value):
    return pltpu.with_memory_space_constraint(value, pltpu.VMEM)


def call(kernel, outs, scratch, far, *args):
    spaces = [pltpu.VMEM] * (len(args) - far) + [pl.ANY] * far
    return pl.pallas_call(
        kernel,
        out_shape=outs,
        in_specs=[pl.BlockSpec(memory_space=space) for space in spaces],
        out_specs=[pl.BlockSpec(memory_space=pltpu.VMEM)] * len(outs),
        scratch_shapes=scratch,
        compiler_params=pltpu.CompilerParams(vmem_limit_bytes=VMEM_LIMIT),
    )(*args)


def per_device(vectors, codes, codebook):
    width, row_count = vectors.shape
    sub_count = codes.shape[0]
    sub_width = width // sub_count
    centroid_count = codebook.shape[0]
    dp_count = lax.axis_size("dp")
    total_width = width * DIMS
    half, thin = 2 * width, width // 2
    high_masks = [4 << bit for bit in range(2, dp_count.bit_length() - 1)]

    book = codebook.T
    book_other, codes_other = swap(book, 2), swap(codes.astype(jnp.int16), 2)
    vectors_core = swap(vectors, 1)
    own_cross, own_vectors = call(
        functools.partial(own_cross_kernel, sub_width),
        [pltpu.VMEM((width, half), jnp.float32), pltpu.VMEM((half, row_count), jnp.bfloat16)],
        [pltpu.VMEM((width, row_count), jnp.float32)],
        0,
        vectors, near(vectors_core), codes, book,
    )
    own_cross, vectors_late = lax.optimization_barrier((own_cross, vectors))
    held = call(
        functools.partial(other_cross_kernel, sub_width),
        [pltpu.VMEM((thin, half), jnp.float32)] * 4,
        [pltpu.VMEM((half, half), jnp.float32), pltpu.VMEM((width, row_count), jnp.float32)],
        0,
        near(own_vectors), near(own_cross), near(codes_other), near(book_other),
    )
    vectors_pair = swap(vectors_late, 2)
    vectors_last = swap(vectors_pair, 1)

    piece = held[0] + swap(held[1], 4) + swap(held[2], 8) + swap(held[3], 12)
    for mask in high_masks[:-1]:
        piece = piece + swap(piece, mask)
    received = swap(piece, high_masks[-1])
    own_pair, own_piece = call(
        code_kernel,
        [pltpu.VMEM((2 * thin + TAIL, half), jnp.int16), pltpu.VMEM((thin + TAIL, half), jnp.int16)],
        [],
        0,
        *map(near, (piece, received, swap(piece, 1), swap(received, 1))),
    )
    pairs = [swap_by_core(own_pair, one, two) for one, two in ROUNDS]
    last = swap(own_piece, LAST)
    gathered = [own_pair, *pairs, *(swap(pair, 1) for pair in pairs), last, swap(last, 1)]

    columns = width + sub_count
    columns += -columns % LANES
    rotation, *sums = call(
        functools.partial(refit_kernel, sub_width),
        [floats(width, total_width)] + [pltpu.VMEM((centroid_count // 4, columns), jnp.float32)] * 4,
        [
            pltpu.VMEM((total_width, total_width), jnp.float32),
            pltpu.VMEM((2, 2, total_width, total_width), jnp.bfloat16),
            pltpu.VMEM((total_width, total_width), jnp.bfloat16),
            pltpu.VMEM((total_width, row_count), jnp.bfloat16),
            pltpu.VMEM((columns, row_count), jnp.bfloat16),
            pltpu.VMEM((centroid_count, columns), jnp.float32),
            pltpu.SemaphoreType.DMA((4,)),
        ],
        4,
        *map(near, gathered), codes, vectors, near(vectors_core), near(vectors_pair), near(vectors_last),
    )
    held = sums[0] + swap(sums[1], 4) + swap(sums[2], 8) + swap(sums[3], 12)
    received = jnp.zeros_like(held)
    for step, mask in enumerate(reversed(high_masks)):
        if step:
            held = held + received
        middle = held.shape[0] // 2
        held, received = held[:middle], swap(held[middle:], mask)
    (new_codebook,) = call(
        functools.partial(finish_kernel, sub_width),
        [floats(centroid_count // dp_count, width)],
        [],
        0,
        near(held), near(received),
    )
    return rotation, new_codebook


def solution(mesh):
    placed = (P("dim", "dp"), P("dim", "dp"), P(None, "dim"))
    return jax.shard_map(
        per_device,
        mesh=mesh,
        in_specs=placed,
        out_specs=(P("dim", None), P("dp", "dim")),
        check_vma=False,
    )
```

```python
import functools

import jax
import jax.numpy as jnp
from jax import lax
from jax.experimental import pallas as pl
from jax.experimental.pallas import tpu as pltpu
from jax.sharding import PartitionSpec as P

NS_STEPS = 4
DIMS = 4
LANES = 128
TAIL = 16
TINY = 1e-30
ROUNDS = ((4, 8), (2, 12), (10, 6))
LAST = 14
VMEM_LIMIT = 56 * 1024 * 1024


def swap(value, mask):
    count = lax.axis_size("dp") * lax.axis_size("dim")
    return lax.ppermute(value, ("dp", "dim"), [(i, i ^ mask) for i in range(count)])


def swap_by_core(value, one, two):
    count = lax.axis_size("dp") * lax.axis_size("dim")
    return lax.ppermute(value, ("dp", "dim"), [(i, i ^ (two if i & 1 else one)) for i in range(count)])


def place():
    dim = lax.axis_index("dim")
    dp = lax.axis_index("dp")
    return dim & 1, dim >> 1, dp & 3, dp >> 2


def split(value):
    high = value.astype(jnp.bfloat16)
    low = (value - high.astype(jnp.float32)).astype(jnp.bfloat16)
    return high, low


def dot_t(a, b):
    return lax.dot_general(a, b, (((1,), (1,)), ((), ())), preferred_element_type=jnp.float32)


def dot(a, b):
    return jnp.dot(a, b, preferred_element_type=jnp.float32)


def decode(codes_ref, book_ref, sub_width, write):
    sub_count, row_count = codes_ref.shape
    codes = codes_ref[...].astype(jnp.int32)
    width = sub_count * sub_width
    sublane = lax.broadcasted_iota(jnp.int32, (8, row_count), 0)
    for first in range(0, width, 8):
        one, two = first // sub_width, (first + 7) // sub_width
        index = jnp.broadcast_to(codes[one : one + 1, :], (8, row_count))
        if two != one:
            later = jnp.broadcast_to(codes[two : two + 1, :], (8, row_count))
            index = jnp.where(sublane < two * sub_width - first, index, later)
        book = book_ref[first : first + 8, :].astype(jnp.float32)
        parts = []
        for start in range(0, row_count, LANES):
            at = index[:, start : start + LANES]
            inner = at & (LANES - 1)
            value = jnp.take_along_axis(book[:, :LANES], inner, axis=1, mode="promise_in_bounds")
            for level in range(LANES, book.shape[1], LANES):
                other = jnp.take_along_axis(
                    book[:, level : level + LANES], inner, axis=1, mode="promise_in_bounds"
                )
                value = jnp.where(at >= level, other, value)
            parts.append(value)
        write(first, jnp.concatenate(parts, axis=1))


def decoded_rows(codes, book, sub_width, rows):
    def write(row, value):
        rows[row : row + 8, :] = value

    decode(codes, book, sub_width, write)
    return rows[...].astype(jnp.bfloat16)


def own_cross_kernel(sub_width, v0, v1, codes, book, cross, vectors, rows):
    core, _, _, _ = place()
    width = v0.shape[0]
    for k, v in enumerate((v0, v1)):
        vectors[pl.ds(pl.multiple_of((core ^ k) * width, 16), width), :] = v[...]
    cross[...] = dot_t(decoded_rows(codes, book, sub_width, rows), vectors[...])


def other_cross_kernel(sub_width, vectors, own, codes, book, *rest):
    outs, (both, rows) = rest[:4], rest[4:]
    _, pair, quarter, _ = place()
    width = own.shape[0]
    thin = width // 2
    both[pl.ds(pl.multiple_of(pair * width, 8), width), :] = own[...]
    other = dot_t(decoded_rows(codes, book, sub_width, rows), vectors[...])
    both[pl.ds(pl.multiple_of((1 - pair) * width, 8), width), :] = other
    for k, out in enumerate(outs):
        out[...] = both[pl.ds(pl.multiple_of((quarter ^ k) * thin, 8), thin), :]


def code_kernel(kept, received, kept_other, received_other, both, mine):
    core, _, _, _ = place()
    count = kept.shape[0]
    exponents = []
    for k, (one, two) in enumerate(((kept, received), (kept_other, received_other))):
        total = one[...] + two[...]
        top = jnp.maximum(jnp.max(jnp.abs(total), axis=0, keepdims=True), TINY)
        exponent = jnp.ceil(jnp.log2(top))
        scaled = jnp.round(total * jnp.exp2(15.0 - exponent))
        coded = jnp.clip(scaled, -32767.0, 32767.0).astype(jnp.int32).astype(jnp.int16)
        exponents.append(jnp.broadcast_to(exponent, (TAIL, total.shape[1])).astype(jnp.int32))
        both[pl.ds(pl.multiple_of((core ^ k) * count, TAIL), count), :] = coded
        if k == 0:
            mine[:count, :] = coded
    row = lax.broadcasted_iota(jnp.int32, exponents[0].shape, 0)
    both[2 * count :, :] = jnp.where((row < TAIL // 2) == (core == 0), *exponents).astype(jnp.int16)
    mine[count:, :] = exponents[0].astype(jnp.int16)


def decoded_piece(ref, first, count, half):
    tail = ref[ref.shape[0] - TAIL :, :].astype(jnp.int32).astype(jnp.float32)
    exponent = tail[half * (TAIL // 2) : half * (TAIL // 2) + 1]
    coded = ref[first : first + count, :].astype(jnp.int32).astype(jnp.float32)
    return coded * jnp.exp2(exponent - 15.0)


def gram_blocks(size, high, write):
    count = high.shape[0] // size
    for i in range(count):
        a = pl.ds(i * size, size)
        for j in range(i, count):
            block = dot_t(high[a, :], high[pl.ds(j * size, size), :]).astype(jnp.bfloat16)
            write(i, j, block)
            if i != j:
                write(j, i, block.T)


def refit_kernel(sub_width, *refs):
    pairs, singles, codes, sources = refs[:7], refs[7:9], refs[9], refs[10:14]
    rotation_out, outs = refs[14], refs[15:19]
    current, highs, low, gram, vectors, rotated, total, arrived = refs[19:]
    core, pair, quarter, high_part = place()
    dp_count = lax.axis_size("dp")
    thin, half = singles[0].shape[0] - TAIL, singles[0].shape[1]
    width, size = 2 * thin, current.shape[0]
    block = 2 * LANES
    own = (pair * 2 + core) * width

    copies = []
    for k, source in enumerate(sources):
        at = ((pair ^ (k >> 1)) * 2 + (core ^ (k & 1))) * width
        rows = pl.ds(pl.multiple_of(at, 16), width)
        copies.append(pltpu.make_async_copy(source, vectors.at[rows, :], arrived.at[k]))
        copies[k].start()

    def place_piece(mask, c, ref, part):
        p, q = pair ^ (mask >> 1 & 1), quarter ^ (mask >> 2)
        row = ((q >> 1) * 2 + c) * width + (q & 1) * thin
        rows, columns = pl.ds(pl.multiple_of(row, 8), thin), pl.ds(pl.multiple_of(p * half, LANES), half)
        current[rows, columns] = decoded_piece(ref, part * thin, thin, part)

    masks = [0] + [jnp.where(core == c, one, two) for c in (0, 1) for one, two in ROUNDS]
    for mask, ref in zip(masks, pairs):
        for c in (0, 1):
            place_piece(mask, c, ref, c)
    for k, ref in enumerate(singles):
        place_piece(LAST, core ^ k, ref, 0)
    squares = jnp.zeros((8, size), jnp.float32)
    for row in range(0, size, 8):
        value = current[row : row + 8, :]
        squares = squares + value * value
    scale = 1.0 / jnp.sqrt(jnp.sum(squares))
    for row in range(0, size, block):
        value = current[row : row + block, :] * scale
        current[row : row + block, :] = value
        highs[0, row : row + block, :] = value.astype(jnp.bfloat16)

    def step(iteration):
        high, later = highs.at[iteration % 2], highs.at[(iteration + 1) % 2]

        def write(i, j, value):
            gram[pl.ds(i * block, block), pl.ds(j * block, block)] = value

        gram_blocks(block, high, write)
        for row in range(0, size, block):
            rows = pl.ds(row, block)
            value = 1.5 * current[rows, :] - 0.5 * dot(gram[rows, :], high[...])
            current[rows, :] = value
            later[rows, :], low[rows, :] = split(value)

    for iteration in range(NS_STEPS - 1):
        step(iteration)
    high = highs.at[(NS_STEPS - 1) % 2]
    rows = pl.ds(pl.multiple_of(own, 16), width)
    stacked = highs.at[NS_STEPS % 2]

    def thin_product(product, a_high, a_low):
        stacked[:width, :], stacked[width : 2 * width, :] = a_high, a_low
        with_high = product(stacked[: 2 * width, :], high[...])
        return with_high[:width] + (with_high[width:] + product(stacked[:width, :], low[...]))

    own_gram = thin_product(dot_t, high[rows, :], low[rows, :])
    update = thin_product(dot, *split(own_gram))
    rotation = 1.5 * current[rows, :] - 0.5 * update
    rotation_out[...] = rotation

    for copy in copies:
        copy.wait()
    sub_count, row_count = codes.shape
    rotated[:width, :] = dot(rotation.astype(jnp.bfloat16), vectors[...]).astype(jnp.bfloat16)
    rotated[width:, :] = jnp.ones((rotated.shape[0] - width, row_count), jnp.bfloat16)

    centroid_count, columns = total.shape
    owner_rows = centroid_count // dp_count
    quarter_rows = centroid_count // 4
    row = lax.broadcasted_iota(jnp.int32, (centroid_count, LANES), 0)
    position = row // quarter_rows
    inner = row % quarter_rows
    level = (((inner // owner_rows) ^ high_part) * 4 + (position ^ quarter)) * owner_rows + inner % owner_rows
    level = jnp.concatenate([level] * (row_count // LANES), axis=1)
    column = lax.broadcasted_iota(jnp.int32, (8, columns), 1)
    subspace = jnp.where(column < width, column // sub_width, column - width)
    subspace = jnp.broadcast_to(subspace[:1], total.shape)
    for m in range(sub_count):
        onehot = (codes[m : m + 1, :] == level).astype(jnp.float32).astype(jnp.bfloat16)
        sums = dot_t(onehot, rotated[...])
        total[...] = jnp.where(subspace == m, sums, total[...] if m else 0.0)
    for k, out in enumerate(outs):
        out[...] = total[k * quarter_rows : (k + 1) * quarter_rows, :]


def finish_kernel(sub_width, kept, received, out):
    total = kept[...] + received[...]
    width = out.shape[1]
    row = lax.broadcasted_iota(jnp.int32, (total.shape[1], width), 0)
    column = lax.broadcasted_iota(jnp.int32, (total.shape[1], width), 1)
    spread = (row == width + column // sub_width).astype(jnp.float32)
    counts = jnp.dot(total, spread, precision=lax.Precision.HIGHEST)
    out[...] = total[:, :width] / jnp.maximum(counts, 1.0)


def floats(*shape):
    return jax.ShapeDtypeStruct(shape, jnp.float32)


def near(value):
    return pltpu.with_memory_space_constraint(value, pltpu.VMEM)


def call(kernel, outs, scratch, far, *args):
    spaces = [pltpu.VMEM] * (len(args) - far) + [pl.ANY] * far
    return pl.pallas_call(
        kernel,
        out_shape=outs,
        in_specs=[pl.BlockSpec(memory_space=space) for space in spaces],
        out_specs=[pl.BlockSpec(memory_space=pltpu.VMEM)] * len(outs),
        scratch_shapes=scratch,
        compiler_params=pltpu.CompilerParams(vmem_limit_bytes=VMEM_LIMIT),
    )(*args)


def per_device(vectors, codes, codebook):
    width, row_count = vectors.shape
    sub_count = codes.shape[0]
    sub_width = width // sub_count
    centroid_count = codebook.shape[0]
    dp_count = lax.axis_size("dp")
    total_width = width * DIMS
    half, thin = 2 * width, width // 2
    high_masks = [4 << bit for bit in range(2, dp_count.bit_length() - 1)]

    book = codebook.T
    book_other, codes_other = swap(book, 2), swap(codes.astype(jnp.int16), 2)
    vectors_core = swap(vectors, 1)
    own_cross, own_vectors = call(
        functools.partial(own_cross_kernel, sub_width),
        [pltpu.VMEM((width, half), jnp.float32), pltpu.VMEM((half, row_count), jnp.bfloat16)],
        [pltpu.VMEM((width, row_count), jnp.float32)],
        0,
        vectors, near(vectors_core), codes, book,
    )
    own_cross, vectors_late = lax.optimization_barrier((own_cross, vectors))
    held = call(
        functools.partial(other_cross_kernel, sub_width),
        [pltpu.VMEM((thin, half), jnp.float32)] * 4,
        [pltpu.VMEM((half, half), jnp.float32), pltpu.VMEM((width, row_count), jnp.float32)],
        0,
        near(own_vectors), near(own_cross), near(codes_other), near(book_other),
    )
    vectors_pair = swap(vectors_late, 2)
    vectors_last = swap(vectors_pair, 1)

    piece = held[0] + swap(held[1], 4) + swap(held[2], 8) + swap(held[3], 12)
    for mask in high_masks[:-1]:
        piece = piece + swap(piece, mask)
    received = swap(piece, high_masks[-1])
    own_pair, own_piece = call(
        code_kernel,
        [pltpu.VMEM((2 * thin + TAIL, half), jnp.int16), pltpu.VMEM((thin + TAIL, half), jnp.int16)],
        [],
        0,
        *map(near, (piece, received, swap(piece, 1), swap(received, 1))),
    )
    pairs = [swap_by_core(own_pair, one, two) for one, two in ROUNDS]
    last = swap(own_piece, LAST)
    gathered = [own_pair, *pairs, *(swap(pair, 1) for pair in pairs), last, swap(last, 1)]

    columns = width + sub_count
    columns += -columns % LANES
    rotation, *sums = call(
        functools.partial(refit_kernel, sub_width),
        [floats(width, total_width)] + [pltpu.VMEM((centroid_count // 4, columns), jnp.float32)] * 4,
        [
            pltpu.VMEM((total_width, total_width), jnp.float32),
            pltpu.VMEM((2, total_width, total_width), jnp.bfloat16),
            pltpu.VMEM((total_width, total_width), jnp.bfloat16),
            pltpu.VMEM((total_width, total_width), jnp.bfloat16),
            pltpu.VMEM((total_width, row_count), jnp.bfloat16),
            pltpu.VMEM((columns, row_count), jnp.bfloat16),
            pltpu.VMEM((centroid_count, columns), jnp.float32),
            pltpu.SemaphoreType.DMA((4,)),
        ],
        4,
        *map(near, gathered), codes, vectors, near(vectors_core), near(vectors_pair), near(vectors_last),
    )
    held = sums[0] + swap(sums[1], 4) + swap(sums[2], 8) + swap(sums[3], 12)
    received = jnp.zeros_like(held)
    for step, mask in enumerate(reversed(high_masks)):
        if step:
            held = held + received
        middle = held.shape[0] // 2
        held, received = held[:middle], swap(held[middle:], mask)
    (new_codebook,) = call(
        functools.partial(finish_kernel, sub_width),
        [floats(centroid_count // dp_count, width)],
        [],
        0,
        near(held), near(received),
    )
    return rotation, new_codebook


def solution(mesh):
    placed = (P("dim", "dp"), P("dim", "dp"), P(None, "dim"))
    return jax.shard_map(
        per_device,
        mesh=mesh,
        in_specs=placed,
        out_specs=(P("dim", None), P("dp", "dim")),
        check_vma=False,
    )
```

```python
import functools

import jax
import jax.numpy as jnp
from jax import lax
from jax.experimental import pallas as pl
from jax.experimental.pallas import tpu as pltpu
from jax.sharding import PartitionSpec as P

NS_STEPS = 4
DIMS = 4
LANES = 128
TAIL = 16
TINY = 1e-30
ROUNDS = ((4, 8), (2, 12), (10, 6))
LAST = 14
VMEM_LIMIT = 56 * 1024 * 1024


def swap(value, mask):
    count = lax.axis_size("dp") * lax.axis_size("dim")
    return lax.ppermute(value, ("dp", "dim"), [(i, i ^ mask) for i in range(count)])


def swap_by_core(value, one, two):
    count = lax.axis_size("dp") * lax.axis_size("dim")
    return lax.ppermute(value, ("dp", "dim"), [(i, i ^ (two if i & 1 else one)) for i in range(count)])


def place():
    dim = lax.axis_index("dim")
    dp = lax.axis_index("dp")
    return dim & 1, dim >> 1, dp & 3, dp >> 2


def split(value):
    high = value.astype(jnp.bfloat16)
    low = (value - high.astype(jnp.float32)).astype(jnp.bfloat16)
    return high, low


def dot_t(a, b):
    return lax.dot_general(a, b, (((1,), (1,)), ((), ())), preferred_element_type=jnp.float32)


def dot(a, b):
    return jnp.dot(a, b, preferred_element_type=jnp.float32)


def decode(codes_ref, book_ref, sub_width, write):
    sub_count, row_count = codes_ref.shape
    codes = codes_ref[...].astype(jnp.int32)
    width = sub_count * sub_width
    sublane = lax.broadcasted_iota(jnp.int32, (8, row_count), 0)
    for first in range(0, width, 8):
        one, two = first // sub_width, (first + 7) // sub_width
        index = jnp.broadcast_to(codes[one : one + 1, :], (8, row_count))
        if two != one:
            later = jnp.broadcast_to(codes[two : two + 1, :], (8, row_count))
            index = jnp.where(sublane < two * sub_width - first, index, later)
        book = book_ref[first : first + 8, :].astype(jnp.float32)
        parts = []
        for start in range(0, row_count, LANES):
            at = index[:, start : start + LANES]
            inner = at & (LANES - 1)
            value = jnp.take_along_axis(book[:, :LANES], inner, axis=1, mode="promise_in_bounds")
            for level in range(LANES, book.shape[1], LANES):
                other = jnp.take_along_axis(
                    book[:, level : level + LANES], inner, axis=1, mode="promise_in_bounds"
                )
                value = jnp.where(at >= level, other, value)
            parts.append(value)
        write(first, jnp.concatenate(parts, axis=1))


def decoded_rows(codes, book, sub_width, rows):
    def write(row, value):
        rows[row : row + 8, :] = value

    decode(codes, book, sub_width, write)
    return rows[...].astype(jnp.bfloat16)


def own_cross_kernel(sub_width, v0, v1, codes, book, cross, vectors, rows):
    core, _, _, _ = place()
    width = v0.shape[0]
    for k, v in enumerate((v0, v1)):
        vectors[pl.ds(pl.multiple_of((core ^ k) * width, 16), width), :] = v[...]
    cross[...] = dot_t(decoded_rows(codes, book, sub_width, rows), vectors[...])


def other_cross_kernel(sub_width, vectors, own, codes, book, *rest):
    outs, (both, rows) = rest[:4], rest[4:]
    _, pair, quarter, _ = place()
    width = own.shape[0]
    thin = width // 2
    both[pl.ds(pl.multiple_of(pair * width, 8), width), :] = own[...]
    other = dot_t(decoded_rows(codes, book, sub_width, rows), vectors[...])
    both[pl.ds(pl.multiple_of((1 - pair) * width, 8), width), :] = other
    for k, out in enumerate(outs):
        out[...] = both[pl.ds(pl.multiple_of((quarter ^ k) * thin, 8), thin), :]


def code_kernel(kept, received, kept_other, received_other, both, mine):
    core, _, _, _ = place()
    count = kept.shape[0]
    exponents = []
    for k, (one, two) in enumerate(((kept, received), (kept_other, received_other))):
        total = one[...] + two[...]
        top = jnp.maximum(jnp.max(jnp.abs(total), axis=0, keepdims=True), TINY)
        exponent = jnp.ceil(jnp.log2(top))
        scaled = jnp.round(total * jnp.exp2(15.0 - exponent))
        coded = jnp.clip(scaled, -32767.0, 32767.0).astype(jnp.int32).astype(jnp.int16)
        exponents.append(jnp.broadcast_to(exponent, (TAIL, total.shape[1])).astype(jnp.int32))
        both[pl.ds(pl.multiple_of((core ^ k) * count, TAIL), count), :] = coded
        if k == 0:
            mine[:count, :] = coded
    row = lax.broadcasted_iota(jnp.int32, exponents[0].shape, 0)
    both[2 * count :, :] = jnp.where((row < TAIL // 2) == (core == 0), *exponents).astype(jnp.int16)
    mine[count:, :] = exponents[0].astype(jnp.int16)


def decoded_piece(ref, first, count, half):
    tail = ref[ref.shape[0] - TAIL :, :].astype(jnp.int32).astype(jnp.float32)
    exponent = tail[half * (TAIL // 2) : half * (TAIL // 2) + 1]
    coded = ref[first : first + count, :].astype(jnp.int32).astype(jnp.float32)
    return coded * jnp.exp2(exponent - 15.0)


def gram_blocks(size, high, write):
    count = high.shape[0] // size
    for i in range(count):
        a = pl.ds(i * size, size)
        for j in range(i, count):
            block = dot_t(high[a, :], high[pl.ds(j * size, size), :]).astype(jnp.bfloat16)
            write(i, j, block)
            if i != j:
                write(j, i, block.T)


def refit_kernel(sub_width, *refs):
    pairs, singles, codes, sources = refs[:7], refs[7:9], refs[9], refs[10:14]
    rotation_out, outs = refs[14], refs[15:19]
    current, highs, low, gram, vectors, rotated, total, arrived = refs[19:]
    core, pair, quarter, high_part = place()
    dp_count = lax.axis_size("dp")
    thin, half = singles[0].shape[0] - TAIL, singles[0].shape[1]
    width, size = 2 * thin, current.shape[0]
    block = 2 * LANES
    own = (pair * 2 + core) * width

    copies = []
    for k, source in enumerate(sources):
        at = ((pair ^ (k >> 1)) * 2 + (core ^ (k & 1))) * width
        rows = pl.ds(pl.multiple_of(at, 16), width)
        copies.append(pltpu.make_async_copy(source, vectors.at[rows, :], arrived.at[k]))
        copies[k].start()

    def place_piece(mask, c, ref, part):
        p, q = pair ^ (mask >> 1 & 1), quarter ^ (mask >> 2)
        row = ((q >> 1) * 2 + c) * width + (q & 1) * thin
        rows, columns = pl.ds(pl.multiple_of(row, 8), thin), pl.ds(pl.multiple_of(p * half, LANES), half)
        current[rows, columns] = decoded_piece(ref, part * thin, thin, part)

    masks = [0] + [jnp.where(core == c, one, two) for c in (0, 1) for one, two in ROUNDS]
    for mask, ref in zip(masks, pairs):
        for c in (0, 1):
            place_piece(mask, c, ref, c)
    for k, ref in enumerate(singles):
        place_piece(LAST, core ^ k, ref, 0)
    squares = jnp.zeros((8, size), jnp.float32)
    for row in range(0, size, 8):
        value = current[row : row + 8, :]
        squares = squares + value * value
    scale = 1.0 / jnp.sqrt(jnp.sum(squares))
    for row in range(0, size, block):
        value = current[row : row + block, :] * scale
        current[row : row + block, :] = value
        highs[0, row : row + block, :] = value.astype(jnp.bfloat16)

    def step(iteration):
        high, later = highs.at[iteration % 2], highs.at[(iteration + 1) % 2]

        def write(i, j, value):
            gram[pl.ds(i * block, block), pl.ds(j * block, block)] = value

        gram_blocks(block, high, write)
        for row in range(0, size, block):
            rows = pl.ds(row, block)
            value = 1.5 * current[rows, :] - 0.5 * dot(gram[rows, :], high[...])
            current[rows, :] = value
            later[rows, :], low[rows, :] = split(value)

    for iteration in range(NS_STEPS - 1):
        step(iteration)
    high = highs.at[(NS_STEPS - 1) % 2]
    rows = pl.ds(pl.multiple_of(own, 16), width)
    stacked = highs.at[NS_STEPS % 2]

    def thin_product(product, a_high, a_low):
        stacked[:width, :], stacked[width : 2 * width, :] = a_high, a_low
        with_high = product(stacked[: 2 * width, :], high[...])
        return with_high[:width] + (with_high[width:] + product(stacked[:width, :], low[...]))

    own_gram = thin_product(dot_t, high[rows, :], low[rows, :])
    update = thin_product(dot, *split(own_gram))
    rotation = 1.5 * current[rows, :] - 0.5 * update
    rotation_out[...] = rotation

    for copy in copies:
        copy.wait()
    sub_count, row_count = codes.shape
    rotated[:width, :] = dot(rotation.astype(jnp.bfloat16), vectors[...]).astype(jnp.bfloat16)
    rotated[width:, :] = jnp.ones((rotated.shape[0] - width, row_count), jnp.bfloat16)

    centroid_count, columns = total.shape
    owner_rows = centroid_count // dp_count
    quarter_rows = centroid_count // 4
    row = lax.broadcasted_iota(jnp.int32, (centroid_count, LANES), 0)
    position = row // quarter_rows
    inner = row % quarter_rows
    level = (((inner // owner_rows) ^ high_part) * 4 + (position ^ quarter)) * owner_rows + inner % owner_rows
    level = jnp.concatenate([level] * (row_count // LANES), axis=1)
    column = lax.broadcasted_iota(jnp.int32, (8, columns), 1)
    subspace = jnp.where(column < width, column // sub_width, column - width)
    subspace = jnp.broadcast_to(subspace[:1], total.shape)
    for m in range(sub_count):
        onehot = (codes[m : m + 1, :] == level).astype(jnp.float32).astype(jnp.bfloat16)
        sums = dot_t(onehot, rotated[...])
        total[...] = jnp.where(subspace == m, sums, total[...] if m else 0.0)
    for k, out in enumerate(outs):
        out[...] = total[k * quarter_rows : (k + 1) * quarter_rows, :]


def finish_kernel(sub_width, kept, received, out):
    total = kept[...] + received[...]
    width = out.shape[1]
    row = lax.broadcasted_iota(jnp.int32, (total.shape[1], width), 0)
    column = lax.broadcasted_iota(jnp.int32, (total.shape[1], width), 1)
    spread = (row == width + column // sub_width).astype(jnp.float32).astype(jnp.bfloat16)
    upper = jnp.floor(total * (1.0 / 256.0))
    lower = total - 256.0 * upper
    counts = 256.0 * dot(upper.astype(jnp.bfloat16), spread) + dot(lower.astype(jnp.bfloat16), spread)
    out[...] = total[:, :width] / jnp.maximum(counts, 1.0)


def floats(*shape):
    return jax.ShapeDtypeStruct(shape, jnp.float32)


def near(value):
    return pltpu.with_memory_space_constraint(value, pltpu.VMEM)


def call(kernel, outs, scratch, far, *args):
    spaces = [pltpu.VMEM] * (len(args) - far) + [pl.ANY] * far
    return pl.pallas_call(
        kernel,
        out_shape=outs,
        in_specs=[pl.BlockSpec(memory_space=space) for space in spaces],
        out_specs=[pl.BlockSpec(memory_space=pltpu.VMEM)] * len(outs),
        scratch_shapes=scratch,
        compiler_params=pltpu.CompilerParams(vmem_limit_bytes=VMEM_LIMIT),
    )(*args)


def per_device(vectors, codes, codebook):
    width, row_count = vectors.shape
    sub_count = codes.shape[0]
    sub_width = width // sub_count
    centroid_count = codebook.shape[0]
    dp_count = lax.axis_size("dp")
    total_width = width * DIMS
    half, thin = 2 * width, width // 2
    high_masks = [4 << bit for bit in range(2, dp_count.bit_length() - 1)]

    book = codebook.T
    book_other, codes_other = swap(book, 2), swap(codes.astype(jnp.int16), 2)
    vectors_core = swap(vectors, 1)
    own_cross, own_vectors = call(
        functools.partial(own_cross_kernel, sub_width),
        [pltpu.VMEM((width, half), jnp.float32), pltpu.VMEM((half, row_count), jnp.bfloat16)],
        [pltpu.VMEM((width, row_count), jnp.float32)],
        0,
        vectors, near(vectors_core), codes, book,
    )
    own_cross, vectors_late = lax.optimization_barrier((own_cross, vectors))
    held = call(
        functools.partial(other_cross_kernel, sub_width),
        [pltpu.VMEM((thin, half), jnp.float32)] * 4,
        [pltpu.VMEM((half, half), jnp.float32), pltpu.VMEM((width, row_count), jnp.float32)],
        0,
        near(own_vectors), near(own_cross), near(codes_other), near(book_other),
    )
    vectors_pair = swap(vectors_late, 2)
    vectors_last = swap(vectors_pair, 1)

    piece = held[0] + swap(held[1], 4) + swap(held[2], 8) + swap(held[3], 12)
    for mask in high_masks[:-1]:
        piece = piece + swap(piece, mask)
    received = swap(piece, high_masks[-1])
    own_pair, own_piece = call(
        code_kernel,
        [pltpu.VMEM((2 * thin + TAIL, half), jnp.int16), pltpu.VMEM((thin + TAIL, half), jnp.int16)],
        [],
        0,
        *map(near, (piece, received, swap(piece, 1), swap(received, 1))),
    )
    pairs = [swap_by_core(own_pair, one, two) for one, two in ROUNDS]
    last = swap(own_piece, LAST)
    gathered = [own_pair, *pairs, *(swap(pair, 1) for pair in pairs), last, swap(last, 1)]

    columns = width + sub_count
    columns += -columns % LANES
    rotation, *sums = call(
        functools.partial(refit_kernel, sub_width),
        [floats(width, total_width)] + [pltpu.VMEM((centroid_count // 4, columns), jnp.float32)] * 4,
        [
            pltpu.VMEM((total_width, total_width), jnp.float32),
            pltpu.VMEM((2, total_width, total_width), jnp.bfloat16),
            pltpu.VMEM((total_width, total_width), jnp.bfloat16),
            pltpu.VMEM((total_width, total_width), jnp.bfloat16),
            pltpu.VMEM((total_width, row_count), jnp.bfloat16),
            pltpu.VMEM((columns, row_count), jnp.bfloat16),
            pltpu.VMEM((centroid_count, columns), jnp.float32),
            pltpu.SemaphoreType.DMA((4,)),
        ],
        4,
        *map(near, gathered), codes, vectors, near(vectors_core), near(vectors_pair), near(vectors_last),
    )
    held = sums[0] + swap(sums[1], 4) + swap(sums[2], 8) + swap(sums[3], 12)
    received = jnp.zeros_like(held)
    for step, mask in enumerate(reversed(high_masks)):
        if step:
            held = held + received
        middle = held.shape[0] // 2
        held, received = held[:middle], swap(held[middle:], mask)
    (new_codebook,) = call(
        functools.partial(finish_kernel, sub_width),
        [floats(centroid_count // dp_count, width)],
        [],
        0,
        near(held), near(received),
    )
    return rotation, new_codebook


def solution(mesh):
    placed = (P("dim", "dp"), P("dim", "dp"), P(None, "dim"))
    return jax.shard_map(
        per_device,
        mesh=mesh,
        in_specs=placed,
        out_specs=(P("dim", None), P("dp", "dim")),
        check_vma=False,
    )
```
